256 devices in a mesh: dp: 32 (over z_lo, y, core), fsdp: 8 (over z_hi, x).
Axes of the slice: x: 4, y: 4, z: 8 (z_hi: 2, z_lo: 4; z = z_hi * 4 + z_lo), core: 2. Of those that a mesh axis runs over, the one named last changes fastest.
Arguments:
- clip: bfloat16 [1, 128, 256, 1024], P(None, 'dp', 'fsdp'), may hold values from -6 to 6
- space_gain: float32 [1024], replicated, may hold values from 0.5 to 1.5
- space_qkv: bfloat16 [1024, 3072], P('fsdp'), may hold values from -2 to 2
- space_out: bfloat16 [1024, 1024], P('fsdp'), may hold values from -0.1875 to 0.1875
- mlp_gain: float32 [1024], replicated, may hold values from 0.5 to 1.5
- mlp_up: bfloat16 [1024, 4096], P('fsdp'), may hold values from -0.1875 to 0.1875
- mlp_down: bfloat16 [4096, 1024], P('fsdp'), may hold values from -0.09375 to 0.09375
- time_gain: float32 [1024], replicated, may hold values from 0.5 to 1.5
- time_qkv: bfloat16 [1024, 3072], P('fsdp'), may hold values from -2 to 2
- time_out: bfloat16 [1024, 1024], P('fsdp'), may hold values from -0.1875 to 0.1875
Outputs:
- encoded: bfloat16 [1, 128, 256, 1024], P(None, 'dp', 'fsdp')
The draws below stay inside these ranges and needn't reach their ends.
All inputs are finite; a program needn't handle non-finite values.
Results may differ from the reference program's by a relative error of at most 0.017.
Values may be sent and summed in bfloat16 or wider, within the bound.
No kernel may reach another device: no remote copies, remote signals or barrier semaphores. Data moves between devices by JAX's collectives and lax.ppermute only.
A program may use at most 128 MiB of HBM per device.

```python
import jax
import jax.numpy as jnp
from jax import lax

D = 1024
HEADS = 16
FF = 4096
CLIPS = 1
FRAMES = 128
PATCHES = 256


def mixed_weights(key, strength):
    first_key, second_key, third_key, fourth_key = jax.random.split(key, 4)
    base = jax.random.normal(first_key, (D, D), jnp.float32)
    other = jax.random.normal(second_key, (D, D), jnp.float32)
    values = jax.random.normal(third_key, (D, D), jnp.float32)
    power = jax.random.uniform(fourth_key, (HEADS,), jnp.float32, 0.5, 1.0)
    head_scale = jnp.repeat(strength ** power, D // HEADS)[None, :]
    query = base * head_scale / jnp.sqrt(D * 1.0)
    keys = jnp.sqrt(1.0) * other * head_scale / jnp.sqrt(D * 1.0)
    return jnp.clip(jnp.concatenate([query, keys, values / jnp.sqrt(D * 1.0)], axis=1), -2.0, 2.0)


def draw_space_qkv(key, part):
    key = jax.random.fold_in(key, 11)
    weights = mixed_weights(key, 1.0)
    return weights.astype(jnp.bfloat16)


def draw_time_qkv(key, part):
    key = jax.random.fold_in(key, 23)
    weights = mixed_weights(key, 1.0)
    return weights.astype(jnp.bfloat16)


def levels(key, extent, pieces, least, high):
    level, own = 1.0, jax.random.fold_in(key, 6)
    for dim, blocks in pieces:
        heights = jnp.exp(jax.random.uniform(jax.random.fold_in(own, dim), (blocks,), jnp.float32, least / len(pieces), high / len(pieces)))
        level = level * jnp.repeat(heights, extent[dim] // blocks).reshape([-1 if axis == dim else 1 for axis in range(len(extent))])
    return level


def normal_values(own_key, extent, scale, bound, shards=(), held_as=jnp.bfloat16):
    values = scale * jax.random.normal(own_key, extent, jnp.float32)
    if shards:
        values = values * levels(own_key, extent, shards, -0.22, 0.18)
    return jnp.clip(values, -bound, bound).astype(held_as)


def setup_inputs(seed: int = 0) -> dict:
    seeds = jax.random.split(jax.random.key(seed), 11)
    return {
        "clip": normal_values(seeds[0], (CLIPS, FRAMES, PATCHES, D), 1.0, 6.0, ((1, 32), (2, 8))),
        "space_gain": jnp.clip(jax.random.uniform(seeds[1], (D,), jnp.float32, 0.5, 1.5), 0.5, 1.5),
        "space_qkv": draw_space_qkv(jax.random.fold_in(seeds[10], 71), 0),
        "space_out": normal_values(seeds[3], (D, D), D ** -0.5, 0.1875, ((0, 8),)),
        "mlp_gain": jnp.clip(jax.random.uniform(seeds[4], (D,), jnp.float32, 0.5, 1.5), 0.5, 1.5),
        "mlp_up": normal_values(seeds[5], (D, FF), D ** -0.5, 0.1875, ((0, 8),)),
        "mlp_down": normal_values(seeds[6], (FF, D), FF ** -0.5, 0.09375, ((0, 8),)),
        "time_gain": jnp.clip(jax.random.uniform(seeds[7], (D,), jnp.float32, 0.5, 1.5), 0.5, 1.5),
        "time_qkv": draw_time_qkv(jax.random.fold_in(seeds[10], 71), 0),
        "time_out": normal_values(seeds[9], (D, D), D ** -0.5, 0.1875, ((0, 8),)),
    }


def layer_norm(values, gain):
    wide = values.astype(jnp.float32)
    centre = lax.optimization_barrier(jnp.mean(wide, axis=-1, keepdims=True))
    spread = lax.optimization_barrier(jnp.mean((wide - centre) * (wide - centre), axis=-1, keepdims=True))
    return ((wide - centre) * lax.rsqrt(spread + 1e-06) * gain).astype(jnp.bfloat16)

def heads_attend(packed):
    length = packed.shape[0]
    width = packed.shape[1] // 3
    head_size = width // HEADS
    query = packed[:, :width].astype(jnp.float32).reshape(length, HEADS, head_size)
    keys = packed[:, width:2 * width].astype(jnp.float32).reshape(length, HEADS, head_size)
    values = packed[:, 2 * width:].astype(jnp.float32).reshape(length, HEADS, head_size)
    scores = jnp.einsum('qhd,khd->hqk', query, keys) * head_size ** (-0.5)
    top = lax.optimization_barrier(jnp.max(scores, axis=-1, keepdims=True))
    weights = jnp.exp(scores - top)
    probs = (weights / lax.optimization_barrier(jnp.sum(weights, axis=-1, keepdims=True))).astype(jnp.bfloat16)
    mixed = jnp.einsum('hqk,khd->qhd', probs.astype(jnp.float32), values)
    return mixed.reshape(length, width).astype(jnp.bfloat16)

def reference(clip, space_gain, space_qkv, space_out, mlp_gain, mlp_up, mlp_down, time_gain, time_qkv, time_out):
    rows = clip.reshape(-1, D)
    normed = layer_norm(rows, space_gain)
    packed = jnp.dot(normed, space_qkv, preferred_element_type=jnp.float32).astype(jnp.bfloat16)
    framed = packed.reshape(CLIPS * FRAMES, PATCHES, 3 * D)
    space_att = lax.map(heads_attend, framed).reshape(-1, D)
    first = (rows.astype(jnp.float32) + jnp.dot(space_att, space_out, preferred_element_type=jnp.float32)).astype(jnp.bfloat16)
    inner = jnp.dot(layer_norm(first, mlp_gain), mlp_up, preferred_element_type=jnp.float32)
    hidden = jax.nn.gelu(inner).astype(jnp.bfloat16)
    second = (first.astype(jnp.float32) + jnp.dot(hidden, mlp_down, preferred_element_type=jnp.float32)).astype(jnp.bfloat16)
    time_norm = layer_norm(second, time_gain)
    time_packed = jnp.dot(time_norm, time_qkv, preferred_element_type=jnp.float32).astype(jnp.bfloat16)
    series = time_packed.reshape(CLIPS, FRAMES, PATCHES, 3 * D).transpose(0, 2, 1, 3).reshape(CLIPS * PATCHES, FRAMES, 3 * D)
    time_att = lax.map(heads_attend, series).reshape(CLIPS, PATCHES, FRAMES, D).transpose(0, 2, 1, 3).reshape(-1, D)
    encoded = (second.astype(jnp.float32) + jnp.dot(time_att, time_out, preferred_element_type=jnp.float32)).astype(jnp.bfloat16)
    return encoded.reshape(CLIPS, FRAMES, PATCHES, D)
```

```python
import functools

import jax
import jax.numpy as jnp
from jax import lax
from jax.experimental import pallas as pl
from jax.experimental.pallas import tpu as pltpu
from jax.sharding import PartitionSpec as P

BF = jnp.bfloat16
F32 = jnp.float32
AXES = ("dp", "fsdp")
PAIRS = 4
HALF = 512


def shift(v, x=0, y=0, z=0, c=0):
    pairs = []
    for sx in range(4):
        for sy in range(4):
            for sz in range(8):
                for sc in range(2):
                    tx, ty, tz, tc = (sx + x) % 4, (sy + y) % 4, (sz + z) % 8, (sc + c) % 2
                    here = (((sz % 4) * 4 + sy) * 2 + sc) * 8 + (sz // 4) * 4 + sx
                    there = (((tz % 4) * 4 + ty) * 2 + tc) * 8 + (tz // 4) * 4 + tx
                    pairs.append((here, there))
    return lax.ppermute(v, AXES, pairs)


def x_ring(near, far):
    rows = near.shape[0]
    both = jnp.concatenate([near, far], axis=0)
    from_left = shift(both, x=1)
    from_right = shift(both, x=-1)
    far_near = shift(from_left[:rows], x=1)
    far_far = shift(from_right[rows:], x=-1)
    return both, from_right, far_near, far_far, from_left


def y_ring(mine):
    rows = mine.shape[0] // 2
    from_below = shift(mine, y=1)
    from_above = shift(mine, y=-1)
    two_low = shift(from_below[:rows], y=1)
    two_high = shift(from_above[rows:], y=-1)
    return mine, from_above, two_low, two_high, from_below


def gather_group(alpha, beta_part):
    ra, rb = alpha.shape[0], beta_part.shape[0]
    near = jnp.concatenate([alpha, beta_part], axis=0)
    rows = ra + rb
    far = shift(near, z=4)
    both, right, two_near, two_far, left = x_ring(near, far)
    cut = lambda a, k: a[k * rows + ra : (k + 1) * rows]
    share = jnp.concatenate(
        [cut(both, 0), cut(right, 0), two_near[ra:], cut(left, 0),
         cut(both, 1), cut(right, 1), two_far[ra:], cut(left, 1)], axis=0)
    return (both, right, two_near, two_far, left), y_ring(share)


def norm_rows(wide, gain):
    centre = jnp.mean(wide, axis=-1, keepdims=True)
    off = wide - centre
    spread = jnp.mean(off * off, axis=-1, keepdims=True)
    return (off * lax.rsqrt(spread + 1e-06) * gain).astype(BF)


def x_pieces(refs, rows):
    both, right, two_near, two_far, left = refs
    return {
        (0, 0): (both, 0), (0, 1): (both, rows),
        (1, 0): (right, 0), (1, 1): (right, rows),
        (2, 0): (two_near, 0), (2, 1): (two_far, 0),
        (3, 0): (left, 0), (3, 1): (left, rows),
    }


def y_pieces(refs, rows):
    mine, above, two_low, two_high, below = refs
    found = {}
    for rz in range(2):
        for rx in range(4):
            at = (rz * 4 + rx) * rows
            found[0, rz, rx] = (mine, at)
            found[1, rz, rx] = (above, at)
            found[2, rz, rx] = (two_low, at) if rz == 0 else (two_high, at - 4 * rows)
            found[3, rz, rx] = (below, at)
    return found


def block_of(place, rx, rz):
    x, zh = place[0], place[1]
    return lax.rem(zh + rz, 2) * 4 + lax.rem(x + rx, 4)


def attend_kernel(seqs, place, tokens, gain, *refs):
    xs, ys = refs[:5], refs[5:10]
    out, wqkv, wout, packed, att, sems = refs[10:]
    copies = []

    def start(src, dst):
        copy = pltpu.make_async_copy(src, dst, sems.at[len(copies)])
        copy.start()
        copies.append(copy)

    for (ry, rz, rx), (ref, at) in y_pieces(ys, 64).items():
        y = lax.rem(place[2] + ry, 4)
        row = block_of(place, rx, rz) * 128 + lax.rem(y, 2) * 64
        column = lax.div(y, 2) * HALF
        start(ref.at[pl.ds(at, 64)],
              wqkv.at[pl.ds(pl.multiple_of(row, 64), 64), pl.ds(pl.multiple_of(column, HALF), HALF)])
    for (rx, rz), (ref, at) in x_pieces(xs, 320).items():
        block = block_of(place, rx, rz)
        start(ref.at[pl.ds(at, 128)],
              wqkv.at[pl.ds(pl.multiple_of(block * 128, 128), 128), pl.ds(2 * HALF, HALF)])
    need = len(copies)
    for (rx, rz), (ref, at) in x_pieces(xs, 320).items():
        row = pl.multiple_of(block_of(place, rx, rz) * 64, 64)
        for half in range(2):
            start(ref.at[pl.ds(at + 128 + half * 64, 64)],
                  wout.at[pl.ds(row, 64), pl.ds(half * HALF, HALF)])
    normed = norm_rows(tokens[...].astype(F32), gain[...])
    for copy in copies[:need]:
        copy.wait()
    for part in range(3):
        cols = slice(part * HALF, (part + 1) * HALF)
        got = jnp.dot(normed, wqkv[:, cols], preferred_element_type=F32)
        packed[:, cols] = got.astype(BF)
    length = tokens.shape[0] // seqs
    low = lax.broadcasted_iota(jnp.int32, (length, 128), 1) < 64
    for seq in range(seqs):
        rows = slice(seq * length, (seq + 1) * length)
        for pair in range(PAIRS):
            query = packed[rows, pair * 128 : pair * 128 + 128] * 0.125
            keys = packed[rows, HALF + pair * 128 : HALF + pair * 128 + 128]
            values = packed[rows, 2 * HALF + pair * 128 : 2 * HALF + pair * 128 + 128]
            mixed = []
            for mask in (low, jnp.logical_not(low)):
                one = jnp.where(mask, query, jnp.zeros_like(query))
                scores = lax.dot_general(one, keys, (((1,), (1,)), ((), ())), preferred_element_type=F32)
                weights = jnp.exp(scores - jnp.max(scores, axis=-1, keepdims=True))
                total = jnp.sum(weights, axis=-1, keepdims=True)
                probs = (weights / total).astype(BF)
                mixed.append(jnp.dot(probs, values, preferred_element_type=F32))
            att[rows, pair * 128 : pair * 128 + 128] = jnp.where(low, mixed[0], mixed[1]).astype(BF)
    for copy in copies[need:]:
        copy.wait()
    out[...] = jnp.dot(att[...], wout[...], preferred_element_type=F32)


def attend_call(seqs, place, tokens, gain, xs, ys):
    count, width = tokens.shape
    vmem = pl.BlockSpec(memory_space=pltpu.VMEM)
    return pl.pallas_call(
        functools.partial(attend_kernel, seqs),
        out_shape=jax.ShapeDtypeStruct((count, width), F32),
        in_specs=[pl.BlockSpec(memory_space=pltpu.SMEM), vmem, vmem] + [pl.BlockSpec(memory_space=pl.ANY)] * 10,
        out_specs=vmem,
        scratch_shapes=[
            pltpu.VMEM((width, 3 * HALF), BF),
            pltpu.VMEM((HALF, width), BF),
            pltpu.VMEM((count, 3 * HALF), BF),
            pltpu.VMEM((count, HALF), BF),
            pltpu.SemaphoreType.DMA((56,)),
        ],
        compiler_params=pltpu.CompilerParams(vmem_limit_bytes=32 * 1024 * 1024),
        cost_estimate=pl.CostEstimate(flops=1400000000, bytes_accessed=6000000, transcendentals=600000),
    )(place, tokens, gain, *xs, *ys)


def mlp_kernel(place, tokens, own, other, gain, *refs):
    xs, ys = refs[:5], refs[5:10]
    first, out, wup, wdown, hidden, sems = refs[10:]
    copies = []

    def start(src, dst):
        copy = pltpu.make_async_copy(src, dst, sems.at[len(copies)])
        copy.start()
        copies.append(copy)

    for (ry, rz, rx), (ref, at) in y_pieces(ys, 128).items():
        column = lax.rem(place[2] + ry, 4) * HALF
        row = block_of(place, rx, rz) * 128
        start(ref.at[pl.ds(at, 128)],
              wup.at[pl.ds(pl.multiple_of(row, 128), 128), pl.ds(pl.multiple_of(column, HALF), HALF)])
    need = len(copies)
    for (rx, rz), (ref, at) in x_pieces(xs, 640).items():
        row = pl.multiple_of(block_of(place, rx, rz) * 256, 256)
        for half in range(2):
            start(ref.at[pl.ds(at + half * 256, 256)],
                  wdown.at[pl.ds(row, 256), pl.ds(half * HALF, HALF)])
    summed = (tokens[...].astype(F32) + (own[...] + other[...])).astype(BF)
    first[...] = summed
    normed = norm_rows(summed.astype(F32), gain[...])
    for copy in copies[:need]:
        copy.wait()
    for part in range(4):
        cols = slice(part * HALF, (part + 1) * HALF)
        inner = jnp.dot(normed, wup[:, cols], preferred_element_type=F32)
        hidden[:, cols] = jax.nn.gelu(inner, approximate=True).astype(BF)
    for copy in copies[need:]:
        copy.wait()
    for part in range(2):
        cols = slice(part * HALF, (part + 1) * HALF)
        out[:, cols] = jnp.dot(hidden[...], wdown[:, cols], preferred_element_type=F32)


def mlp_call(place, tokens, own, other, gain, xs, ys):
    count, width = tokens.shape
    vmem = pl.BlockSpec(memory_space=pltpu.VMEM)
    return pl.pallas_call(
        mlp_kernel,
        out_shape=(jax.ShapeDtypeStruct((count, width), BF), jax.ShapeDtypeStruct((count, width), F32)),
        in_specs=[pl.BlockSpec(memory_space=pltpu.SMEM)] + [vmem] * 4 + [pl.BlockSpec(memory_space=pl.ANY)] * 10,
        out_specs=(vmem, vmem),
        scratch_shapes=[
            pltpu.VMEM((width, 4 * HALF), BF),
            pltpu.VMEM((4 * HALF, width), BF),
            pltpu.VMEM((count, 4 * HALF), BF),
            pltpu.SemaphoreType.DMA((48,)),
        ],
        compiler_params=pltpu.CompilerParams(vmem_limit_bytes=40 * 1024 * 1024),
        cost_estimate=pl.CostEstimate(flops=2200000000, bytes_accessed=11000000, transcendentals=600000),
    )(place, tokens, own, other, gain, *xs, *ys)


def core_half(c, a, b):
    return jnp.where(c == 0, a, b)


def attend_weights(c, y, qkv, project):
    rows, width = project.shape
    heads = qkv.reshape(rows, 3, 8, 2, 64)
    mine = core_half(c, heads[:, :, :, 0], heads[:, :, :, 1]).reshape(rows, 3, HALF)
    down = core_half(c, project[:64], project[64:])
    alpha = jnp.concatenate([mine[:, 2], down[:, :HALF], down[:, HALF:]], axis=0)
    beta = jnp.concatenate([mine[:, 0], mine[:, 1]], axis=0)
    return alpha, lax.dynamic_slice_in_dim(beta, y * 64, 64, axis=0)


def mlp_weights(c, y, up, down):
    mine = core_half(c, up.reshape(128, 8, 2, 256)[:, :, 0], up.reshape(128, 8, 2, 256)[:, :, 1]).reshape(128, 2048)
    part = lax.dynamic_slice_in_dim(mine, y * HALF, HALF, axis=1)
    low = core_half(c, down[:256], down[256:])
    return jnp.concatenate([low[:, :HALF], low[:, HALF:]], axis=0), part


def both_cores(c, v):
    other = shift(v, c=1)
    return core_half(c, jnp.concatenate([v, other], axis=0), jnp.concatenate([other, v], axis=0))


def body(clip, space_gain, space_qkv, space_out, mlp_gain, mlp_up, mlp_down, time_gain, time_qkv, time_out):
    dp, fs = lax.axis_index("dp"), lax.axis_index("fsdp")
    c, y = lax.rem(dp, 2), lax.rem(lax.div(dp, 2), 4)
    place = jnp.stack([lax.rem(fs, 4), lax.div(fs, 4), y]).astype(jnp.int32)
    width = clip.shape[-1]

    space = gather_group(*attend_weights(c, y, space_qkv, space_out))
    middle = gather_group(*mlp_weights(c, y, mlp_up, mlp_down))
    time = gather_group(*attend_weights(c, y, time_qkv, time_out))

    split = clip.reshape(4, 16, 2, width)
    keep = core_half(c, split[:, :, 0], split[:, :, 1])
    give = core_half(c, split[:, :, 1], split[:, :, 0])
    taken = shift(give, c=1)
    frames = core_half(c, jnp.concatenate([keep, taken], axis=0), jnp.concatenate([taken, keep], axis=0))
    frames = lax.all_to_all(frames, "fsdp", split_axis=0, concat_axis=0, tiled=True)
    frames = frames.transpose(1, 0, 2).reshape(128, width)
    tokens = both_cores(c, frames)

    partial = attend_call(1, place, tokens, space_gain.reshape(1, width), *space)
    first, lowered = mlp_call(place, tokens, partial, shift(partial, c=1), mlp_gain.reshape(1, width), *middle)
    mine = lax.dynamic_slice_in_dim(lowered, c * 128, 128, axis=0)
    away = lax.dynamic_slice_in_dim(lowered, (1 - c) * 128, 128, axis=0)
    kept = lax.dynamic_slice_in_dim(first, c * 128, 128, axis=0)
    second = (kept.astype(F32) + (mine + shift(away, c=1))).astype(BF)

    groups = [[(2 * m + core) * 8 + k for m in range(16) for k in range(8)] for core in range(2)]
    series = lax.all_to_all(second, AXES, split_axis=0, concat_axis=0, tiled=True, axis_index_groups=groups)
    partial = attend_call(2, place, both_cores(c, series), time_gain.reshape(1, width), *time)
    mine = lax.dynamic_slice_in_dim(partial, c * 128, 128, axis=0)
    away = lax.dynamic_slice_in_dim(partial, (1 - c) * 128, 128, axis=0)
    done = (series.astype(F32) + (mine + shift(away, c=1))).astype(BF)
    return lax.all_to_all(done.reshape(1, 128, 1, width), "dp", split_axis=1, concat_axis=2, tiled=True)


def solution(mesh):
    return jax.shard_map(
        body,
        mesh=mesh,
        in_specs=(
            P(None, "dp", "fsdp", None),
            P(),
            P("fsdp", None),
            P("fsdp", None),
            P(),
            P("fsdp", None),
            P("fsdp", None),
            P(),
            P("fsdp", None),
            P("fsdp", None),
        ),
        out_specs=P(None, "dp", "fsdp", None),
        check_vma=False,
    )
```

```python
import functools

import jax
import jax.numpy as jnp
from jax import lax
from jax.experimental import pallas as pl
from jax.experimental.pallas import tpu as pltpu
from jax.sharding import PartitionSpec as P

BF = jnp.bfloat16
F32 = jnp.float32
AXES = ("dp", "fsdp")
PAIRS = 4
HALF = 512


def shift(v, x=0, y=0, z=0, c=0):
    pairs = []
    for sx in range(4):
        for sy in range(4):
            for sz in range(8):
                for sc in range(2):
                    tx, ty, tz, tc = (sx + x) % 4, (sy + y) % 4, (sz + z) % 8, (sc + c) % 2
                    here = (((sz % 4) * 4 + sy) * 2 + sc) * 8 + (sz // 4) * 4 + sx
                    there = (((tz % 4) * 4 + ty) * 2 + tc) * 8 + (tz // 4) * 4 + tx
                    pairs.append((here, there))
    return lax.ppermute(v, AXES, pairs)


def ring(near, far, axis):
    go = lambda v, step: shift(v, **{axis: step})
    near_left, near_right = go(near, 1), go(near, -1)
    near_two = go(near_left, 1)
    far_left, far_right = go(far, 1), go(far, -1)
    far_two = go(far_right, -1)
    return (near, near_right, near_two, near_left), (far, far_right, far_two, far_left)


def after(v, *others):
    return lax.optimization_barrier((v, *others))[0]


def stack_kernel(*refs):
    pieces, out, sems = refs[:4], refs[4], refs[5]
    rows = pieces[0].shape[0]
    copies = [pltpu.make_async_copy(ref, out.at[pl.ds(i * rows, rows)], sems.at[i]) for i, ref in enumerate(pieces)]
    for copy in copies:
        copy.start()
    for copy in copies:
        copy.wait()


def stack(pieces):
    rows, width = pieces[0].shape
    return pl.pallas_call(
        stack_kernel,
        out_shape=jax.ShapeDtypeStruct((4 * rows, width), BF),
        in_specs=[pl.BlockSpec(memory_space=pl.ANY)] * 4,
        out_specs=pl.BlockSpec(memory_space=pl.ANY),
        scratch_shapes=[pltpu.SemaphoreType.DMA((4,))],
        cost_estimate=pl.CostEstimate(flops=0, bytes_accessed=8 * rows * width * 2, transcendentals=0),
    )(*pieces)


def split_attend(c, qkv, project, out):
    source = lax.broadcasted_iota(jnp.int32, (256, 128), 0)
    lane = lax.broadcasted_iota(jnp.int32, (256, 128), 1)
    pick = (source == lane + jnp.where(lane < 64, 0, 64) + c * 64).astype(F32).astype(BF)
    for part in range(3):
        for pair in range(PAIRS):
            block = qkv[:, part * 1024 + pair * 256 : part * 1024 + pair * 256 + 256]
            got = jnp.dot(block, pick, preferred_element_type=F32).astype(BF)
            out[part * 128 : part * 128 + 128, pair * 128 : pair * 128 + 128] = got
    rows = pl.ds(pl.multiple_of(c * 64, 64), 64)
    out[384:448, :] = project[rows, :HALF]
    out[448:512, :] = project[rows, HALF:]


def time_piece_kernel(place, qkv, project, out):
    split_attend(place[3], qkv, project, out)


def piece_kernel(place, qkv, project, up, down, straight, shared):
    y, c = place[2], place[3]
    for block in range(2):
        columns = pl.ds(pl.multiple_of(y * 1024 + block * 512 + c * 256, 256), 256)
        shared[0:128, block * 256 : block * 256 + 256] = up[:, columns]
    shared[128:192, :] = down[pl.ds(pl.multiple_of(c * 256 + y * 64, 64), 64), :HALF]
    straight[512:768, :] = down[pl.ds(pl.multiple_of(c * 256, 256), 256), HALF:]
    split_attend(c, qkv, project, straight)


VMEM = pl.BlockSpec(memory_space=pltpu.VMEM)
SMEM = pl.BlockSpec(memory_space=pltpu.SMEM)
ANY = pl.BlockSpec(memory_space=pl.ANY)


def make_pieces(place, qkv, project, up, down):
    return pl.pallas_call(
        piece_kernel,
        out_shape=(jax.ShapeDtypeStruct((768, HALF), BF), jax.ShapeDtypeStruct((192, HALF), BF)),
        in_specs=[SMEM] + [VMEM] * 4,
        out_specs=(VMEM, VMEM),
        compiler_params=pltpu.CompilerParams(vmem_limit_bytes=16 * 1024 * 1024),
        cost_estimate=pl.CostEstimate(flops=100000000, bytes_accessed=4000000, transcendentals=0),
    )(place, qkv, project, up, down)


def make_time_piece(place, qkv, project):
    return pl.pallas_call(
        time_piece_kernel,
        out_shape=jax.ShapeDtypeStruct((512, HALF), BF),
        in_specs=[SMEM] + [VMEM] * 2,
        out_specs=VMEM,
        compiler_params=pltpu.CompilerParams(vmem_limit_bytes=16 * 1024 * 1024),
        cost_estimate=pl.CostEstimate(flops=100000000, bytes_accessed=2000000, transcendentals=0),
    )(place, qkv, project)


def norm_rows(wide, gain):
    centre = jnp.mean(wide, axis=-1, keepdims=True)
    off = wide - centre
    spread = jnp.mean(off * off, axis=-1, keepdims=True)
    return (off * lax.rsqrt(spread + 1e-06) * gain).astype(BF)


def block_of(place, rx, rz):
    return lax.rem(place[1] + rz, 2) * 4 + lax.rem(place[0] + rx, 4)


def attend_kernel(seqs, place, tokens, gain, *refs):
    pieces = refs[:8]
    out, wqkv, wout, packed, att, sems = refs[8:]
    copies = []

    def start(src, dst):
        copy = pltpu.make_async_copy(src, dst, sems.at[len(copies)])
        copy.start()
        copies.append(copy)

    for part in range(3):
        for i, ref in enumerate(pieces):
            row = pl.multiple_of(block_of(place, i % 4, i // 4) * 128, 128)
            start(ref.at[pl.ds(part * 128, 128)], wqkv.at[pl.ds(row, 128), pl.ds(part * HALF, HALF)])
    need = len(copies)
    for i, ref in enumerate(pieces):
        row = pl.multiple_of(block_of(place, i % 4, i // 4) * 64, 64)
        for half in range(2):
            start(ref.at[pl.ds(384 + half * 64, 64)], wout.at[pl.ds(row, 64), pl.ds(half * HALF, HALF)])
    normed = norm_rows(tokens[...].astype(F32), gain[...])
    count = tokens.shape[0]
    for part in range(3):
        cols = slice(part * HALF, (part + 1) * HALF)
        for copy in copies[part * 8 : part * 8 + 8]:
            copy.wait()
        got = jnp.dot(normed, wqkv[:, cols], preferred_element_type=F32)
        packed[:, cols] = got.astype(BF)
    low = lax.broadcasted_iota(jnp.int32, (count, 128), 1) < 64
    length = count // seqs
    if seqs > 1:
        same = lax.broadcasted_iota(jnp.int32, (count, count), 0) // length == lax.broadcasted_iota(jnp.int32, (count, count), 1) // length
    for pair in range(PAIRS):
        query = packed[:, pair * 128 : pair * 128 + 128] * 0.125
        keys = packed[:, HALF + pair * 128 : HALF + pair * 128 + 128]
        values = packed[:, 2 * HALF + pair * 128 : 2 * HALF + pair * 128 + 128]
        mixed = []
        for mask in (low, jnp.logical_not(low)):
            one = jnp.where(mask, query, jnp.zeros_like(query))
            scores = lax.dot_general(one, keys, (((1,), (1,)), ((), ())), preferred_element_type=F32)
            if seqs > 1:
                scores = jnp.where(same, scores, -1e30)
            weights = jnp.exp(scores - jnp.max(scores, axis=-1, keepdims=True))
            total = jnp.sum(weights, axis=-1, keepdims=True)
            mixed.append(jnp.dot(weights.astype(BF), values, preferred_element_type=F32) * (1.0 / total))
        att[:, pair * 128 : pair * 128 + 128] = jnp.where(low, mixed[0], mixed[1]).astype(BF)
    for copy in copies[need:]:
        copy.wait()
    out[...] = jnp.dot(att[...], wout[...], preferred_element_type=F32)


def attend_call(seqs, place, tokens, gain, pieces):
    count, width = tokens.shape
    return pl.pallas_call(
        functools.partial(attend_kernel, seqs),
        out_shape=jax.ShapeDtypeStruct((count, width), F32),
        in_specs=[SMEM, VMEM, VMEM] + [ANY] * 8,
        out_specs=VMEM,
        scratch_shapes=[
            pltpu.VMEM((width, 3 * HALF), BF),
            pltpu.VMEM((HALF, width), BF),
            pltpu.VMEM((count, 3 * HALF), BF),
            pltpu.VMEM((count, HALF), BF),
            pltpu.SemaphoreType.DMA((40,)),
        ],
        compiler_params=pltpu.CompilerParams(vmem_limit_bytes=32 * 1024 * 1024),
        cost_estimate=pl.CostEstimate(flops=1400000000, bytes_accessed=6000000, transcendentals=600000),
    )(place, tokens, gain, *pieces)


def mlp_kernel(place, tokens, own, other, gain, *refs):
    straight, shared = refs[:8], refs[8:16]
    first, out, wup, wdown, hidden, sems = refs[16:]
    copies = []

    def start(src, dst):
        copy = pltpu.make_async_copy(src, dst, sems.at[len(copies)])
        copy.start()
        copies.append(copy)

    spots = [(i % 4, i // 4, ref, rx) for i, ref in enumerate(shared) for rx in range(4)]
    for ry, rz, ref, rx in spots:
        column = pl.multiple_of(lax.rem(place[2] + ry, 4) * HALF, HALF)
        row = pl.multiple_of(block_of(place, rx, rz) * 128, 128)
        start(ref.at[pl.ds(rx * 192, 128)], wup.at[pl.ds(row, 128), pl.ds(column, HALF)])
    need = len(copies)
    for ry, rz, ref, rx in spots:
        row = pl.multiple_of(block_of(place, rx, rz) * 256 + lax.rem(place[2] + ry, 4) * 64, 64)
        start(ref.at[pl.ds(rx * 192 + 128, 64)], wdown.at[pl.ds(row, 64), pl.ds(0, HALF)])
    for i, ref in enumerate(straight):
        row = pl.multiple_of(block_of(place, i % 4, i // 4) * 256, 256)
        start(ref.at[pl.ds(512, 256)], wdown.at[pl.ds(row, 256), pl.ds(HALF, HALF)])
    summed = (tokens[...].astype(F32) + (own[...] + other[...])).astype(BF)
    first[...] = summed
    normed = norm_rows(summed.astype(F32), gain[...])
    for copy in copies[:need]:
        copy.wait()
    for part in range(4):
        cols = slice(part * HALF, (part + 1) * HALF)
        inner = jnp.dot(normed, wup[:, cols], preferred_element_type=F32)
        hidden[:, cols] = jax.nn.gelu(inner, approximate=True).astype(BF)
    for copy in copies[need:]:
        copy.wait()
    for part in range(2):
        cols = slice(part * HALF, (part + 1) * HALF)
        out[:, cols] = jnp.dot(hidden[...], wdown[:, cols], preferred_element_type=F32)


def mlp_call(place, tokens, own, other, gain, straight, shared):
    count, width = tokens.shape
    return pl.pallas_call(
        mlp_kernel,
        out_shape=(jax.ShapeDtypeStruct((count, width), BF), jax.ShapeDtypeStruct((count, width), F32)),
        in_specs=[SMEM] + [VMEM] * 4 + [ANY] * 16,
        out_specs=(VMEM, VMEM),
        scratch_shapes=[
            pltpu.VMEM((width, 4 * HALF), BF),
            pltpu.VMEM((4 * HALF, width), BF),
            pltpu.VMEM((count, 4 * HALF), BF),
            pltpu.SemaphoreType.DMA((72,)),
        ],
        compiler_params=pltpu.CompilerParams(vmem_limit_bytes=40 * 1024 * 1024),
        cost_estimate=pl.CostEstimate(flops=2200000000, bytes_accessed=11000000, transcendentals=600000),
    )(place, tokens, own, other, gain, *straight, *shared)


def core_half(c, a, b):
    return jnp.where(c == 0, a, b)


def both_cores(c, v):
    other = shift(v, c=1)
    return core_half(c, jnp.concatenate([v, other], axis=0), jnp.concatenate([other, v], axis=0))


def body(clip, space_gain, space_qkv, space_out, mlp_gain, mlp_up, mlp_down, time_gain, time_qkv, time_out):
    dp, fs = lax.axis_index("dp"), lax.axis_index("fsdp")
    c, y = lax.rem(dp, 2), lax.rem(lax.div(dp, 2), 4)
    place = jnp.stack([lax.rem(fs, 4), lax.div(fs, 4), y, c]).astype(jnp.int32)
    width = clip.shape[-1]

    straight, shared = make_pieces(place, space_qkv, space_out, mlp_up, mlp_down)
    shared_near, shared_far = ring(shared, shift(shared, z=4), "x")
    straight_near, straight_far = ring(straight, shift(straight, z=4), "x")
    shared_near, shared_far = ring(stack(shared_near), stack(shared_far), "y")
    time_qkv = after(time_qkv, straight_far[1])
    time_piece = make_time_piece(place, time_qkv, time_out)
    time_near, time_far = ring(time_piece, shift(time_piece, z=4), "x")

    split = clip.reshape(4, 16, 2, width)
    keep = core_half(c, split[:, :, 0], split[:, :, 1])
    give = core_half(c, split[:, :, 1], split[:, :, 0])
    taken = shift(give, c=1)
    frames = core_half(c, jnp.concatenate([keep, taken], axis=0), jnp.concatenate([taken, keep], axis=0))
    frames = lax.all_to_all(frames, "fsdp", split_axis=0, concat_axis=0, tiled=True)
    frames = frames.transpose(1, 0, 2).reshape(128, width)
    tokens = both_cores(c, frames)

    partial = attend_call(1, place, tokens, space_gain.reshape(1, width), straight_near + straight_far)
    first, lowered = mlp_call(place, tokens, partial, shift(partial, c=1), mlp_gain.reshape(1, width),
                              straight_near + straight_far, shared_near + shared_far)
    mine = lax.dynamic_slice_in_dim(lowered, c * 128, 128, axis=0)
    away = lax.dynamic_slice_in_dim(lowered, (1 - c) * 128, 128, axis=0)
    kept = lax.dynamic_slice_in_dim(first, c * 128, 128, axis=0)
    second = (kept.astype(F32) + (mine + shift(away, c=1))).astype(BF)

    groups = [[(2 * m + core) * 8 + k for m in range(16) for k in range(8)] for core in range(2)]
    series = lax.all_to_all(second, AXES, split_axis=0, concat_axis=0, tiled=True, axis_index_groups=groups)
    partial = attend_call(2, place, both_cores(c, series), time_gain.reshape(1, width), time_near + time_far)
    mine = lax.dynamic_slice_in_dim(partial, c * 128, 128, axis=0)
    away = lax.dynamic_slice_in_dim(partial, (1 - c) * 128, 128, axis=0)
    done = (series.astype(F32) + (mine + shift(away, c=1))).astype(BF)
    return lax.all_to_all(done.reshape(1, 128, 1, width), "dp", split_axis=1, concat_axis=2, tiled=True)


def solution(mesh):
    return jax.shard_map(
        body,
        mesh=mesh,
        in_specs=(
            P(None, "dp", "fsdp", None),
            P(),
            P("fsdp", None),
            P("fsdp", None),
            P(),
            P("fsdp", None),
            P("fsdp", None),
            P(),
            P("fsdp", None),
            P("fsdp", None),
        ),
        out_specs=P(None, "dp", "fsdp", None),
        check_vma=False,
    )
```

```python
import functools

import jax
import jax.numpy as jnp
from jax import lax
from jax.experimental import pallas as pl
from jax.experimental.pallas import tpu as pltpu
from jax.sharding import PartitionSpec as P

BF = jnp.bfloat16
F32 = jnp.float32
AXES = ("dp", "fsdp")
ROWS = 128
HALF = 512
VMEM = pl.BlockSpec(memory_space=pltpu.VMEM)
SMEM = pl.BlockSpec(memory_space=pltpu.SMEM)
ANY = pl.BlockSpec(memory_space=pl.ANY)
BIG = pltpu.CompilerParams(vmem_limit_bytes=56 * 1024 * 1024)


def device(x, y, z, c):
    return (((z % 4) * 4 + y) * 2 + c) * 8 + (z // 4) * 4 + x


def chips():
    return [(x, y, z, c) for x in range(4) for y in range(4) for z in range(8) for c in range(2)]


def shift(v, x=0, y=0, z=0, c=0):
    pairs = [
        (device(a, b, d, e), device((a + x) % 4, (b + y) % 4, (d + z) % 8, (e + c) % 2)) for a, b, d, e in chips()
    ]
    return lax.ppermute(v, AXES, pairs)


def swap_chips(v):
    return lax.ppermute(v, AXES, [(device(a, b, d, e), device(a, b ^ 1, d, e)) for a, b, d, e in chips()])


def norm_rows(wide, gain):
    centre = jnp.mean(wide, axis=-1, keepdims=True)
    off = wide - centre
    spread = jnp.mean(off * off, axis=-1, keepdims=True)
    return (off * lax.rsqrt(spread + 1e-06) * gain).astype(BF)


def start_copies(pairs, sems):
    copies = []
    for i, (src, dst) in enumerate(pairs):
        copy = pltpu.make_async_copy(src, dst, sems.at[i])
        copy.start()
        copies.append(copy)
    return copies


def aligned(offset, size, unit):
    return pl.ds(pl.multiple_of(offset, unit), size)


def shares_kernel(place, sqkv, sproject, up, down, tqkv, tproject, near, space, time,
                  sheads, srows, ups, downs, theads, trows, sems):
    y, c, zl, quarter = place[2], place[3], place[4], place[5]
    half = aligned(c * 64, 64, 64)
    pairs = [(sqkv, sheads), (sproject.at[half], srows)]
    for i in range(2):
        pairs.append((up.at[:, aligned((2 * zl + i) * 512 + quarter * 128, 128, 128)], ups.at[i]))
    pairs.append((down.at[aligned(quarter * 128 + zl * 32, 32, 32)], downs))
    for part in range(3):
        pairs.append((tqkv.at[:, aligned(part * 1024 + y * 256, 256, 256)], theads.at[part]))
    pairs.append((tproject.at[half, aligned(y * 256, 256, 256)], trows))
    for copy in start_copies(pairs, sems):
        copy.wait()

    source = lax.broadcasted_iota(jnp.int32, (512, 128), 0)
    lane = lax.broadcasted_iota(jnp.int32, (512, 128), 1)
    pick = (source == lane + jnp.where(lane < 64, 0, 192) + quarter * 64).astype(F32).astype(BF)
    for pair in range(2):
        at = pair * 128
        for part in range(3):
            block = sheads[:, part * 1024 + pair * 512 : part * 1024 + pair * 512 + 512]
            got = jnp.dot(block, pick, preferred_element_type=F32).astype(BF)
            for ref in (near, space):
                ref[at : at + 128, part * 128 : part * 128 + 128] = got
        for ref in (near, space):
            ref[at : at + 64, 384:512] = srows[:, pair * 256 : pair * 256 + 128]
            ref[at + 64 : at + 128, 384:512] = srows[:, pair * 256 + 128 : pair * 256 + 256]
    for ref in (near, space):
        ref[256:320, :] = srows[:, 512:]
    for i in range(2):
        near[320:384, i * 128 : i * 128 + 128] = ups[i, :64]
        near[320:384, 256 + i * 128 : 384 + i * 128] = ups[i, 64:]
        near[384 + i * 32 : 416 + i * 32, :] = downs[:, i * HALF : (i + 1) * HALF]

    source = lax.broadcasted_iota(jnp.int32, (256, 128), 0)
    lane = lax.broadcasted_iota(jnp.int32, (256, 128), 1)
    pick = (source == lane + jnp.where(lane < 64, 0, 64) + c * 64).astype(F32).astype(BF)
    for part in range(3):
        time[:, part * 128 : part * 128 + 128] = jnp.dot(theads[part], pick, preferred_element_type=F32).astype(BF)
    time[0:64, 384:512] = trows[:, :128]
    time[64:128, 384:512] = trows[:, 128:]


def make_shares(place, *weights):
    return pl.pallas_call(
        shares_kernel,
        out_shape=[jax.ShapeDtypeStruct((rows, HALF), BF) for rows in (448, 320, 128)],
        in_specs=[SMEM] + [ANY] * 6,
        out_specs=[VMEM] * 3,
        scratch_shapes=[
            pltpu.VMEM((128, 3072), BF),
            pltpu.VMEM((64, 1024), BF),
            pltpu.VMEM((2, 128, 128), BF),
            pltpu.VMEM((32, 1024), BF),
            pltpu.VMEM((3, 128, 256), BF),
            pltpu.VMEM((64, 256), BF),
            pltpu.SemaphoreType.DMA((9,)),
        ],
        compiler_params=BIG,
        cost_estimate=pl.CostEstimate(flops=120000000, bytes_accessed=2500000, transcendentals=0),
    )(place, *weights)


def stack_kernel(a, b, c, d, out, sems):
    for copy in start_copies([(ref.at[pl.ds(320, 128)], out.at[pl.ds(i * 128, 128)]) for i, ref in enumerate((a, b, c, d))], sems):
        copy.wait()


def stack(pieces):
    return pl.pallas_call(
        stack_kernel,
        out_shape=jax.ShapeDtypeStruct((512, HALF), BF),
        in_specs=[ANY] * 4,
        out_specs=VMEM,
        scratch_shapes=[pltpu.SemaphoreType.DMA((4,))],
        compiler_params=BIG,
        cost_estimate=pl.CostEstimate(flops=0, bytes_accessed=1000000, transcendentals=0),
    )(*pieces)


def attend_pair(query, keys, values, seqs):
    count = query.shape[0]
    low = lax.broadcasted_iota(jnp.int32, (count, 128), 1) < 64
    mixed = []
    for mask in (low, jnp.logical_not(low)):
        one = jnp.where(mask, query, jnp.zeros_like(query))
        scores = lax.dot_general(one, keys, (((1,), (1,)), ((), ())), preferred_element_type=F32)
        if seqs > 1:
            length = count // seqs
            row = lax.broadcasted_iota(jnp.int32, (count, count), 0) // length
            column = lax.broadcasted_iota(jnp.int32, (count, count), 1) // length
            scores = jnp.where(row == column, scores, -1e30)
        weights = jnp.exp(scores - jnp.max(scores, axis=-1, keepdims=True))
        total = jnp.sum(weights, axis=-1, keepdims=True)
        mixed.append(jnp.dot(weights.astype(BF), values, preferred_element_type=F32) * (1.0 / total))
    return jnp.where(low, mixed[0], mixed[1]).astype(BF)


def space_kernel(place, own, other, far, far_other, gain, *refs):
    pieces = refs[:8]
    base, away, over, tokens, wqkv, wout, packed, att, sems = refs[8:]
    blocks = [
        (lax.rem(place[1] + step // 4, 2) * 4 + lax.rem(place[0] + step, 4), ref) for step, ref in enumerate(pieces)
    ]
    pairs = []
    for pair in range(2):
        for block, ref in blocks:
            pairs.append((ref.at[pl.ds(pair * 128, 128), pl.ds(0, 384)],
                          wqkv.at[aligned(block * 128, 128, 128), pl.ds(pair * 384, 384)]))
    copies = start_copies(pairs, sems)
    odd = lax.rem(place[0] + place[2], 2)
    late = []
    for slot in range(4):
        ways = []
        for parity in range(2):
            block, ref = blocks[(slot // 2) * 4 + (slot % 2) * 2 + parity]
            row = aligned(lax.div(block, 2) * 64, 64, 64)
            ways.append([
                pltpu.make_async_copy(src, wout.at[row, pl.ds(column, src.shape[1])], sems.at[16 + slot * 5 + i])
                for i, (src, column) in enumerate(
                    [(ref.at[pl.ds(256, 64), :], 512)]
                    + [(ref.at[pl.ds(k * 64, 64), pl.ds(384, 128)], k * 128) for k in range(4)])
            ])
        for parity in range(2):

            @pl.when(odd == parity)
            def _():
                for copy in ways[parity]:
                    copy.start()

        late.append(ways)
    for i, ref in enumerate((own, other, far, far_other)):
        tokens[i * ROWS : (i + 1) * ROWS, :] = norm_rows(ref[...].astype(F32), gain[...])
    for pair in range(2):
        for copy in copies[pair * 8 : pair * 8 + 8]:
            copy.wait()
        cols = slice(pair * 384, pair * 384 + 384)
        packed[:, cols] = jnp.dot(tokens[...], wqkv[:, cols], preferred_element_type=F32).astype(BF)
        for frame in range(2):
            rows = slice(frame * 256, frame * 256 + 256)
            query, keys, values = (packed[rows, pair * 384 + i * 128 : pair * 384 + i * 128 + 128] for i in range(3))
            att[rows, pair * 128 : pair * 128 + 128] = attend_pair(query * 0.125, keys, values, 1)
    for ways in late:
        for parity in range(2):

            @pl.when(odd == parity)
            def _():
                for copy in ways[parity]:
                    copy.wait()

    row = lambda i: jnp.dot(att[i * ROWS : (i + 1) * ROWS, :], wout[...], preferred_element_type=F32)
    away[:ROWS, :] = row(1)
    away[ROWS:, :] = row(3)
    over[...] = row(2)
    base[...] = own[...].astype(F32) + row(0)


def wide(rows):
    return jax.ShapeDtypeStruct((rows, 1024), F32)


def space_call(place, tokens, gain, pieces):
    return pl.pallas_call(
        space_kernel,
        out_shape=[wide(ROWS), wide(2 * ROWS), wide(ROWS)],
        in_specs=[SMEM] + [VMEM] * 5 + [ANY] * 8,
        out_specs=[VMEM] * 3,
        scratch_shapes=[
            pltpu.VMEM((4 * ROWS, 1024), BF),
            pltpu.VMEM((1024, 768), BF),
            pltpu.VMEM((256, 1024), BF),
            pltpu.VMEM((4 * ROWS, 768), BF),
            pltpu.VMEM((4 * ROWS, 256), BF),
            pltpu.SemaphoreType.DMA((36,)),
        ],
        compiler_params=BIG,
        cost_estimate=pl.CostEstimate(flops=1400000000, bytes_accessed=6000000, transcendentals=600000),
    )(place, *tokens, gain, *pieces)


def norm_kernel(base, came, over, gain, first, normed):
    summed = (base[...] + came[:ROWS, :] + over[...].astype(F32)).astype(BF)
    first[...] = summed
    normed[...] = norm_rows(summed.astype(F32), gain[...])


def norm_call(base, came, over, gain):
    return pl.pallas_call(
        norm_kernel,
        out_shape=[jax.ShapeDtypeStruct((ROWS, 1024), BF)] * 2,
        in_specs=[VMEM] * 4,
        out_specs=[VMEM] * 2,
        cost_estimate=pl.CostEstimate(flops=2000000, bytes_accessed=2500000, transcendentals=0),
    )(base, came, over, gain)


def mlp_kernel(place, first, own, other, far, far_other, *refs):
    pieces = refs[:8]
    base, away, over, tokens, wup, wdown, hidden, sems = refs[8:]
    pairs, lower = [], []
    for step, ref in enumerate(pieces):
        z = lax.rem(place[1] * 4 + place[4] + step, 8)
        zl = lax.rem(z, 4)
        for rx in range(4):
            block = lax.div(z, 4) * 4 + lax.rem(place[0] + rx, 4)
            for i in range(2):
                pairs.append((ref.at[pl.ds(rx * 128, 64), pl.ds(i * 256, 256)],
                              wup.at[aligned(block * 128 + i * 64, 64, 64), aligned(zl * 256, 256, 256)]))
                lower.append((ref.at[pl.ds(rx * 128 + 64 + i * 32, 32), :],
                              wdown.at[aligned(block * 128 + zl * 32, 32, 32), pl.ds(i * HALF, HALF)]))
    copies = start_copies(pairs + lower, sems)
    for i, ref in enumerate((own, other, far, far_other)):
        tokens[i * ROWS : (i + 1) * ROWS, :] = ref[...]
    for copy in copies[: len(pairs)]:
        copy.wait()
    for part in range(2):
        cols = slice(part * HALF, (part + 1) * HALF)
        inner = jnp.dot(tokens[...], wup[:, cols], preferred_element_type=F32)
        hidden[:, cols] = jax.nn.gelu(inner, approximate=True).astype(BF)
    for copy in copies[len(pairs) :]:
        copy.wait()
    row = lambda i: jnp.dot(hidden[i * ROWS : (i + 1) * ROWS, :], wdown[...], preferred_element_type=F32)
    away[:ROWS, :] = row(1)
    away[ROWS:, :] = row(3)
    over[...] = row(2)
    base[...] = first[...].astype(F32) + row(0)


def mlp_call(place, first, tokens, pieces):
    return pl.pallas_call(
        mlp_kernel,
        out_shape=[wide(ROWS), wide(2 * ROWS), wide(ROWS)],
        in_specs=[SMEM] + [VMEM] * 5 + [ANY] * 8,
        out_specs=[VMEM] * 3,
        scratch_shapes=[
            pltpu.VMEM((4 * ROWS, 1024), BF),
            pltpu.VMEM((1024, 1024), BF),
            pltpu.VMEM((1024, 1024), BF),
            pltpu.VMEM((4 * ROWS, 1024), BF),
            pltpu.SemaphoreType.DMA((128,)),
        ],
        compiler_params=BIG,
        cost_estimate=pl.CostEstimate(flops=2200000000, bytes_accessed=9000000, transcendentals=600000),
    )(place, first, *tokens, *pieces)


def time_kernel(place, own, other, gain, shared, base, away, tokens, wqkv, wout, packed, att, sems):
    spots = [(y, x, rz) for y in range(4) for x in range(4) for rz in range(2)]
    pairs, lower = [], []
    for y, x, rz in spots:
        block = lax.rem(place[1] + rz, 2) * 4 + x
        at = ((y * 4 + x) * 2 + rz) * 128
        pairs.append((shared.at[pl.ds(at, 128), pl.ds(0, 384)], wqkv.at[aligned(block * 128, 128, 128), pl.ds(y * 384, 384)]))
        for i in range(2):
            lower.append((shared.at[pl.ds(at + i * 64, 64), pl.ds(384, 128)],
                          wout.at[aligned(block * 64, 64, 64), pl.ds(y * 256 + i * 128, 128)]))
    copies = start_copies(pairs + lower, sems)
    tokens[:ROWS, :] = norm_rows(own[...].astype(F32), gain[...])
    tokens[ROWS:, :] = norm_rows(other[...].astype(F32), gain[...])
    for pair in range(4):
        for copy in copies[pair * 8 : pair * 8 + 8]:
            copy.wait()
        cols = slice(pair * 384, pair * 384 + 384)
        packed[:, cols] = jnp.dot(tokens[...], wqkv[:, cols], preferred_element_type=F32).astype(BF)
        query, keys, values = (packed[:, pair * 384 + i * 128 : pair * 384 + i * 128 + 128] for i in range(3))
        att[:, pair * 128 : pair * 128 + 128] = attend_pair(query * 0.125, keys, values, 2)
    for copy in copies[len(pairs) :]:
        copy.wait()
    away[...] = jnp.dot(att[ROWS:, :], wout[...], preferred_element_type=F32)
    base[...] = own[...].astype(F32) + jnp.dot(att[:ROWS, :], wout[...], preferred_element_type=F32)


def time_call(place, own, other, gain, shared):
    return pl.pallas_call(
        time_kernel,
        out_shape=[wide(ROWS), wide(ROWS)],
        in_specs=[SMEM] + [VMEM] * 3 + [ANY],
        out_specs=[VMEM] * 2,
        scratch_shapes=[
            pltpu.VMEM((2 * ROWS, 1024), BF),
            pltpu.VMEM((1024, 1536), BF),
            pltpu.VMEM((512, 1024), BF),
            pltpu.VMEM((2 * ROWS, 1536), BF),
            pltpu.VMEM((2 * ROWS, 512), BF),
            pltpu.SemaphoreType.DMA((96,)),
        ],
        compiler_params=BIG,
        cost_estimate=pl.CostEstimate(flops=1400000000, bytes_accessed=6000000, transcendentals=600000),
    )(place, own, other, gain, shared)


def body(clip, space_gain, space_qkv, space_out, mlp_gain, mlp_up, mlp_down, time_gain, time_qkv, time_out):
    dp, fs = lax.axis_index("dp"), lax.axis_index("fsdp")
    x, zh, c, y, zl = lax.rem(fs, 4), lax.div(fs, 4), lax.rem(dp, 2), lax.rem(lax.div(dp, 2), 4), lax.div(dp, 8)
    place = jnp.stack([x, zh, y, c, zl, lax.rem(y, 2) * 2 + c]).astype(jnp.int32)
    width = clip.shape[-1]
    gains = [gain.reshape(1, width) for gain in (space_gain, mlp_gain, time_gain)]

    together = lambda *v: lax.optimization_barrier(v)
    planes = [[device(px, py, z, core) for py in range(4) for px in range(4)] for z in range(8) for core in range(2)]
    near, space, time = make_shares(place, space_qkv, space_out, mlp_up, mlp_down, time_qkv, time_out)
    far = shift(space, z=4)
    near = near, shift(near, x=-1), shift(near, x=2), shift(near, x=1)
    split = clip.reshape(4, 16, 2, width)
    keep = jnp.where(c == 0, split[:, :, 0], split[:, :, 1])
    give = jnp.where(c == 0, split[:, :, 1], split[:, :, 0])
    taken = shift(give, c=1)
    frames = jnp.where(c == 0, jnp.concatenate([keep, taken], axis=0), jnp.concatenate([taken, keep], axis=0))
    frames = lax.all_to_all(frames, "fsdp", split_axis=0, concat_axis=0, tiled=True)
    own = frames.transpose(1, 0, 2).reshape(ROWS, width)
    far, *near = together(far, *near)
    far = far, shift(far, x=-1), shift(far, x=2), shift(far, x=1)
    mlp = stack(near)
    over = swap_chips(own)
    up, down = [mlp, shift(mlp, z=1)], [mlp, shift(mlp, z=-1)]
    over, up[1], down[1], time, *far = together(over, up[1], down[1], time, *far)
    time_far = shift(time, z=4)
    up.append(shift(up[1], z=1))
    down.append(shift(down[1], z=-1))
    space = (*near, *far)

    base, away, over = space_call(place, (own, shift(own, c=1), over, shift(over, c=1)), gains[0], space)
    away, time, time_far = together(away, time, time_far)
    shared = lax.all_gather(jnp.concatenate([time, time_far], axis=0), AXES, axis=0, tiled=True, axis_index_groups=planes)
    came = shift(away, c=1)
    came, up[2], down[2] = together(came, up[2], down[2])
    up.append(shift(up[2], z=1))
    down.append(shift(down[2], z=-1))
    over = swap_chips((over + came[ROWS:]).astype(BF))
    over, up[3], down[3] = together(over, up[3], down[3])
    up.append(shift(up[3], z=1))
    first, normed = norm_call(base, came, over, gains[1])
    over = swap_chips(normed)
    base, away, over = mlp_call(place, first, (normed, shift(normed, c=1), over, shift(over, c=1)), down + up[4:0:-1])
    came = shift(away, c=1)
    over = swap_chips((over + came[ROWS:]).astype(BF))
    second = (base + came[:ROWS] + over.astype(F32)).astype(BF)

    groups = [[(2 * m + core) * 8 + k for m in range(16) for k in range(8)] for core in range(2)]
    series = lax.all_to_all(second, AXES, split_axis=0, concat_axis=0, tiled=True, axis_index_groups=groups)
    base, away = time_call(place, series, shift(series, c=1), gains[2], shared)
    done = (base + shift(away, c=1)).astype(BF)
    return lax.all_to_all(done.reshape(1, ROWS, 1, width), "dp", split_axis=1, concat_axis=2, tiled=True)


def solution(mesh):
    return jax.shard_map(
        body,
        mesh=mesh,
        in_specs=(
            P(None, "dp", "fsdp", None),
            P(),
            P("fsdp", None),
            P("fsdp", None),
            P(),
            P("fsdp", None),
            P("fsdp", None),
            P(),
            P("fsdp", None),
            P("fsdp", None),
        ),
        out_specs=P(None, "dp", "fsdp", None),
        check_vma=False,
    )
```

```python
import functools

import jax
import jax.numpy as jnp
from jax import lax
from jax.experimental import pallas as pl
from jax.experimental.pallas import tpu as pltpu
from jax.sharding import PartitionSpec as P

BF = jnp.bfloat16
F32 = jnp.float32
AXES = ("dp", "fsdp")
ROWS = 128
HALF = 512
VMEM = pl.BlockSpec(memory_space=pltpu.VMEM)
SMEM = pl.BlockSpec(memory_space=pltpu.SMEM)
ANY = pl.BlockSpec(memory_space=pl.ANY)
BIG = pltpu.CompilerParams(vmem_limit_bytes=56 * 1024 * 1024)


def device(x, y, z, c):
    return (((z % 4) * 4 + y) * 2 + c) * 8 + (z // 4) * 4 + x


def chips():
    return [(x, y, z, c) for x in range(4) for y in range(4) for z in range(8) for c in range(2)]


def shift(v, x=0, y=0, z=0, c=0):
    pairs = [
        (device(a, b, d, e), device((a + x) % 4, (b + y) % 4, (d + z) % 8, (e + c) % 2)) for a, b, d, e in chips()
    ]
    return lax.ppermute(v, AXES, pairs)


def swap_chips(v):
    return lax.ppermute(v, AXES, [(device(a, b, d, e), device(a, b ^ 1, d, e)) for a, b, d, e in chips()])


def norm_rows(wide, gain):
    centre = jnp.mean(wide, axis=-1, keepdims=True)
    off = wide - centre
    spread = jnp.mean(off * off, axis=-1, keepdims=True)
    return (off * lax.rsqrt(spread + 1e-06) * gain).astype(BF)


def start_copies(pairs, sems):
    copies = []
    for i, (src, dst) in enumerate(pairs):
        copy = pltpu.make_async_copy(src, dst, sems.at[i])
        copy.start()
        copies.append(copy)
    return copies


def aligned(offset, size, unit):
    return pl.ds(pl.multiple_of(offset, unit), size)


def shares_kernel(place, sqkv, sproject, up, down, tqkv, tproject, near, reach,
                  sheads, srows, ups, downs, theads, trows, sems):
    y, c, zl, quarter = place[2], place[3], place[4], place[5]
    half = aligned(c * 64, 64, 64)
    pairs = [(sqkv, sheads), (sproject.at[half], srows)]
    for i in range(2):
        pairs.append((up.at[:, aligned((2 * zl + i) * 512 + quarter * 128, 128, 128)], ups.at[i]))
    pairs.append((down.at[aligned(quarter * 128 + zl * 32, 32, 32)], downs))
    for part in range(3):
        pairs.append((tqkv.at[:, aligned(part * 1024 + y * 256, 256, 256)], theads.at[part]))
    pairs.append((tproject.at[half, aligned(y * 256, 256, 256)], trows))
    for copy in start_copies(pairs, sems):
        copy.wait()

    source = lax.broadcasted_iota(jnp.int32, (512, 128), 0)
    lane = lax.broadcasted_iota(jnp.int32, (512, 128), 1)
    pick = (source == lane + jnp.where(lane < 64, 0, 192) + quarter * 64).astype(F32).astype(BF)
    for pair in range(2):
        at = pair * 128
        for part in range(3):
            block = sheads[:, part * 1024 + pair * 512 : part * 1024 + pair * 512 + 512]
            got = jnp.dot(block, pick, preferred_element_type=F32).astype(BF)
            for ref in (near, reach):
                ref[at : at + 128, part * 128 : part * 128 + 128] = got
        for ref in (near, reach):
            ref[at : at + 64, 384:512] = srows[:, pair * 256 : pair * 256 + 128]
            ref[at + 64 : at + 128, 384:512] = srows[:, pair * 256 + 128 : pair * 256 + 256]
    for ref in (near, reach):
        ref[256:320, :] = srows[:, 512:]
    for i in range(2):
        near[320:448, i * 128 : i * 128 + 128] = ups[i]
    for i in range(4):
        near[320 + i * 32 : 352 + i * 32, 256:512] = downs[:, i * 256 : i * 256 + 256]

    source = lax.broadcasted_iota(jnp.int32, (256, 128), 0)
    lane = lax.broadcasted_iota(jnp.int32, (256, 128), 1)
    pick = (source == lane + jnp.where(lane < 64, 0, 64) + c * 64).astype(F32).astype(BF)
    for part in range(3):
        reach[320:448, part * 128 : part * 128 + 128] = jnp.dot(theads[part], pick, preferred_element_type=F32).astype(BF)
    reach[320:384, 384:512] = trows[:, :128]
    reach[384:448, 384:512] = trows[:, 128:]


def make_shares(place, *weights):
    return pl.pallas_call(
        shares_kernel,
        out_shape=[jax.ShapeDtypeStruct((rows, HALF), BF) for rows in (448, 448)],
        in_specs=[SMEM] + [ANY] * 6,
        out_specs=[VMEM] * 2,
        scratch_shapes=[
            pltpu.VMEM((128, 3072), BF),
            pltpu.VMEM((64, 1024), BF),
            pltpu.VMEM((2, 128, 128), BF),
            pltpu.VMEM((32, 1024), BF),
            pltpu.VMEM((3, 128, 256), BF),
            pltpu.VMEM((64, 256), BF),
            pltpu.SemaphoreType.DMA((9,)),
        ],
        compiler_params=BIG,
        cost_estimate=pl.CostEstimate(flops=120000000, bytes_accessed=2500000, transcendentals=0),
    )(place, *weights)


def stack_kernel(a, b, c, d, out, sems):
    for copy in start_copies([(ref.at[pl.ds(320, 128)], out.at[pl.ds(i * 128, 128)]) for i, ref in enumerate((a, b, c, d))], sems):
        copy.wait()


def stack(pieces):
    return pl.pallas_call(
        stack_kernel,
        out_shape=jax.ShapeDtypeStruct((512, HALF), BF),
        in_specs=[ANY] * 4,
        out_specs=VMEM,
        scratch_shapes=[pltpu.SemaphoreType.DMA((4,))],
        compiler_params=BIG,
        cost_estimate=pl.CostEstimate(flops=0, bytes_accessed=1000000, transcendentals=0),
    )(*pieces)


def attend_pair(query, keys, values, seqs):
    count = query.shape[0]
    low = lax.broadcasted_iota(jnp.int32, (count, 128), 1) < 64
    mixed = []
    for mask in (low, jnp.logical_not(low)):
        one = jnp.where(mask, query, jnp.zeros_like(query))
        scores = lax.dot_general(one, keys, (((1,), (1,)), ((), ())), preferred_element_type=F32)
        if seqs > 1:
            length = count // seqs
            row = lax.broadcasted_iota(jnp.int32, (count, count), 0) // length
            column = lax.broadcasted_iota(jnp.int32, (count, count), 1) // length
            scores = jnp.where(row == column, scores, -1e30)
        weights = jnp.exp(scores - jnp.max(scores, axis=-1, keepdims=True))
        total = jnp.sum(weights, axis=-1, keepdims=True)
        mixed.append(jnp.dot(weights.astype(BF), values, preferred_element_type=F32) * (1.0 / total))
    return jnp.where(low, mixed[0], mixed[1]).astype(BF)


def space_kernel(place, own, other, far, far_other, gain, *refs):
    pieces = refs[:8]
    base, away, over, tokens, wqkv, wout, packed, att, sems = refs[8:]
    blocks = [
        (lax.rem(place[1] + step // 4, 2) * 4 + lax.rem(place[0] + step, 4), ref) for step, ref in enumerate(pieces)
    ]
    pairs = []
    for pair in range(2):
        for block, ref in blocks:
            pairs.append((ref.at[pl.ds(pair * 128, 128), pl.ds(0, 384)],
                          wqkv.at[aligned(block * 128, 128, 128), pl.ds(pair * 384, 384)]))
    copies = start_copies(pairs, sems)
    odd = lax.rem(place[0] + place[2], 2)
    late = []
    for slot in range(4):
        ways = []
        for parity in range(2):
            block, ref = blocks[(slot // 2) * 4 + (slot % 2) * 2 + parity]
            row = aligned(lax.div(block, 2) * 64, 64, 64)
            ways.append([
                pltpu.make_async_copy(src, wout.at[row, pl.ds(column, src.shape[1])], sems.at[16 + slot * 5 + i])
                for i, (src, column) in enumerate(
                    [(ref.at[pl.ds(256, 64), :], 512)]
                    + [(ref.at[pl.ds(k * 64, 64), pl.ds(384, 128)], k * 128) for k in range(4)])
            ])
        for parity in range(2):

            @pl.when(odd == parity)
            def _():
                for copy in ways[parity]:
                    copy.start()

        late.append(ways)
    for i, ref in enumerate((own, other, far, far_other)):
        tokens[i * ROWS : (i + 1) * ROWS, :] = norm_rows(ref[...].astype(F32), gain[...])
    for pair in range(2):
        for copy in copies[pair * 8 : pair * 8 + 8]:
            copy.wait()
        cols = slice(pair * 384, pair * 384 + 384)
        packed[:, cols] = jnp.dot(tokens[...], wqkv[:, cols], preferred_element_type=F32).astype(BF)
        for frame in range(2):
            rows = slice(frame * 256, frame * 256 + 256)
            query, keys, values = (packed[rows, pair * 384 + i * 128 : pair * 384 + i * 128 + 128] for i in range(3))
            att[rows, pair * 128 : pair * 128 + 128] = attend_pair(query * 0.125, keys, values, 1)
    for ways in late:
        for parity in range(2):

            @pl.when(odd == parity)
            def _():
                for copy in ways[parity]:
                    copy.wait()

    row = lambda i: jnp.dot(att[i * ROWS : (i + 1) * ROWS, :], wout[...], preferred_element_type=F32)
    away[:ROWS, :] = row(1)
    away[ROWS:, :] = row(3)
    over[...] = row(2)
    base[...] = own[...].astype(F32) + row(0)


def wide(rows):
    return jax.ShapeDtypeStruct((rows, 1024), F32)


def space_call(place, tokens, gain, pieces):
    return pl.pallas_call(
        space_kernel,
        out_shape=[wide(ROWS), wide(2 * ROWS), wide(ROWS)],
        in_specs=[SMEM] + [VMEM] * 5 + [ANY] * 8,
        out_specs=[VMEM] * 3,
        scratch_shapes=[
            pltpu.VMEM((4 * ROWS, 1024), BF),
            pltpu.VMEM((1024, 768), BF),
            pltpu.VMEM((256, 1024), BF),
            pltpu.VMEM((4 * ROWS, 768), BF),
            pltpu.VMEM((4 * ROWS, 256), BF),
            pltpu.SemaphoreType.DMA((36,)),
        ],
        compiler_params=BIG,
        cost_estimate=pl.CostEstimate(flops=1400000000, bytes_accessed=6000000, transcendentals=600000),
    )(place, *tokens, gain, *pieces)


def norm_kernel(base, came, over, gain, first, normed):
    summed = (base[...] + came[:ROWS, :] + over[...].astype(F32)).astype(BF)
    first[...] = summed
    normed[...] = norm_rows(summed.astype(F32), gain[...])


def norm_call(base, came, over, gain):
    return pl.pallas_call(
        norm_kernel,
        out_shape=[jax.ShapeDtypeStruct((ROWS, 1024), BF)] * 2,
        in_specs=[VMEM] * 4,
        out_specs=[VMEM] * 2,
        cost_estimate=pl.CostEstimate(flops=2000000, bytes_accessed=2500000, transcendentals=0),
    )(base, came, over, gain)


def mlp_kernel(place, first, own, other, far, far_other, *refs):
    pieces, refs = refs[:9], refs[9:]
    base, away, over, tokens, wup, wdown, hidden, sems = refs
    pairs, lower = [], []
    for step in range(8):
        z = lax.rem(place[1] * 4 + place[4] + step, 8)
        zl = lax.rem(z, 4)
        for rx in range(4):
            ref, at = pieces[step], rx * 128
            if step == 4:
                ref, at = pieces[4 + rx // 2 * 4], rx % 2 * 128
            block = lax.div(z, 4) * 4 + lax.rem(place[0] + rx, 4)
            pairs.append((ref.at[pl.ds(at, 128), pl.ds(0, 256)],
                          wup.at[aligned(block * 128, 128, 128), aligned(zl * 256, 256, 256)]))
            lower.append((ref.at[pl.ds(at, 128), pl.ds(256, 256)], wdown.at[block * 4 + zl]))
    copies = start_copies(pairs + lower, sems)
    for i, ref in enumerate((own, other, far, far_other)):
        tokens[i * ROWS : (i + 1) * ROWS, :] = ref[...]
    for copy in copies[: len(pairs)]:
        copy.wait()
    for part in range(2):
        cols = slice(part * HALF, (part + 1) * HALF)
        inner = jnp.dot(tokens[...], wup[:, cols], preferred_element_type=F32)
        hidden[:, cols] = jax.nn.gelu(inner, approximate=True).astype(BF)
    for copy in copies[len(pairs) :]:
        copy.wait()
    for part in range(4):
        cols = slice(part * 256, part * 256 + 256)
        got = jnp.dot(hidden[...], wdown[:, part * 32 : part * 32 + 32, :].reshape(1024, 256), preferred_element_type=F32)
        base[:, cols] = first[:, cols].astype(F32) + got[:ROWS]
        away[:ROWS, cols] = got[ROWS : 2 * ROWS]
        over[:, cols] = got[2 * ROWS : 3 * ROWS]
        away[ROWS:, cols] = got[3 * ROWS :]


def mlp_call(place, first, tokens, pieces):
    return pl.pallas_call(
        mlp_kernel,
        out_shape=[wide(ROWS), wide(2 * ROWS), wide(ROWS)],
        in_specs=[SMEM] + [VMEM] * 5 + [ANY] * 9,
        out_specs=[VMEM] * 3,
        scratch_shapes=[
            pltpu.VMEM((4 * ROWS, 1024), BF),
            pltpu.VMEM((1024, 1024), BF),
            pltpu.VMEM((32, 128, 256), BF),
            pltpu.VMEM((4 * ROWS, 1024), BF),
            pltpu.SemaphoreType.DMA((64,)),
        ],
        compiler_params=BIG,
        cost_estimate=pl.CostEstimate(flops=2200000000, bytes_accessed=9000000, transcendentals=600000),
    )(place, first, *tokens, *pieces)


def time_kernel(place, own, other, gain, shared, base, away, tokens, weights, packed, att, sems):
    pairs = []
    for y in range(4):
        for x in range(4):
            for rz in range(2):
                block = lax.rem(place[1] + rz, 2) * 4 + x
                pairs.append((shared.at[pl.ds(((y * 4 + x) * 2 + rz) * 128, 128)],
                              weights.at[aligned(block * 128, 128, 128), pl.ds(y * HALF, HALF)]))
    copies = start_copies(pairs, sems)
    tokens[:ROWS, :] = norm_rows(own[...].astype(F32), gain[...])
    tokens[ROWS:, :] = norm_rows(other[...].astype(F32), gain[...])
    for pair in range(4):
        for copy in copies[pair * 8 : pair * 8 + 8]:
            copy.wait()
        at = pair * 384
        packed[:, at : at + 384] = jnp.dot(
            tokens[...], weights[:, pair * HALF : pair * HALF + 384], preferred_element_type=F32).astype(BF)
        query, keys, values = (packed[:, at + i * 128 : at + i * 128 + 128] for i in range(3))
        att[:, pair * 128 : pair * 128 + 128] = attend_pair(query * 0.125, keys, values, 2)
    for pair in range(4):
        lanes = slice(pair * HALF + 384, pair * HALF + 512)
        rows = jnp.concatenate([
            jnp.concatenate([weights[block * 128 + i * 64 : block * 128 + i * 64 + 64, lanes] for block in range(8)], axis=0)
            for i in range(2)], axis=1)
        cols = slice(pair * 256, pair * 256 + 256)
        got = jnp.dot(att[...], rows, preferred_element_type=F32)
        base[:, cols] = own[:, cols].astype(F32) + got[:ROWS]
        away[:, cols] = got[ROWS:]


def time_call(place, own, other, gain, shared):
    return pl.pallas_call(
        time_kernel,
        out_shape=[wide(ROWS), wide(ROWS)],
        in_specs=[SMEM] + [VMEM] * 3 + [ANY],
        out_specs=[VMEM] * 2,
        scratch_shapes=[
            pltpu.VMEM((2 * ROWS, 1024), BF),
            pltpu.VMEM((1024, 2048), BF),
            pltpu.VMEM((2 * ROWS, 1536), BF),
            pltpu.VMEM((2 * ROWS, 512), BF),
            pltpu.SemaphoreType.DMA((32,)),
        ],
        compiler_params=BIG,
        cost_estimate=pl.CostEstimate(flops=1400000000, bytes_accessed=6000000, transcendentals=600000),
    )(place, own, other, gain, shared)


def body(clip, space_gain, space_qkv, space_out, mlp_gain, mlp_up, mlp_down, time_gain, time_qkv, time_out):
    dp, fs = lax.axis_index("dp"), lax.axis_index("fsdp")
    x, zh, c, y, zl = lax.rem(fs, 4), lax.div(fs, 4), lax.rem(dp, 2), lax.rem(lax.div(dp, 2), 4), lax.div(dp, 8)
    place = jnp.stack([x, zh, y, c, zl, lax.rem(y, 2) * 2 + c]).astype(jnp.int32)
    width = clip.shape[-1]
    gains = [gain.reshape(1, width) for gain in (space_gain, mlp_gain, time_gain)]

    together = lambda *v: lax.optimization_barrier(v)
    planes = [[device(px, py, z, core) for py in range(4) for px in range(4)] for z in range(8) for core in range(2)]
    near, reach = make_shares(place, space_qkv, space_out, mlp_up, mlp_down, time_qkv, time_out)
    far = shift(reach, z=4)
    near = near, shift(near, x=-1), shift(near, x=2), shift(near, x=1)
    split = clip.reshape(4, 16, 2, width)
    keep = jnp.where(c == 0, split[:, :, 0], split[:, :, 1])
    give = jnp.where(c == 0, split[:, :, 1], split[:, :, 0])
    taken = shift(give, c=1)
    frames = jnp.where(c == 0, jnp.concatenate([keep, taken], axis=0), jnp.concatenate([taken, keep], axis=0))
    frames = lax.all_to_all(frames, "fsdp", split_axis=0, concat_axis=0, tiled=True)
    own = frames.transpose(1, 0, 2).reshape(ROWS, width)
    far, *near = together(far, *near)
    piece = far[:320]
    far = far, shift(piece, x=-1), shift(piece, x=2), shift(piece, x=1)
    mlp = stack(near)
    over = swap_chips(own)
    up, down = [mlp, shift(mlp, z=1)], [mlp, shift(mlp, z=-1)]
    over, up[1], down[1], *far = together(over, up[1], down[1], *far)
    up.append(shift(up[1], z=1))
    down.append(shift(down[1], z=-1))
    space = (*near, *far)
    shared = jnp.concatenate([reach[320:], far[0][320:]], axis=0)
    shared = lax.all_gather(shared, AXES, axis=0, tiled=True, axis_index_groups=planes)

    base, away, over = space_call(place, (own, shift(own, c=1), over, shift(over, c=1)), gains[0], space)
    came = shift(away, c=1)
    over = swap_chips((over + came[ROWS:]).astype(BF))
    over, up[2], down[2] = together(over, up[2], down[2])
    up.append(shift(up[2], z=1))
    down.append(shift(down[2], z=-1))
    first, normed = norm_call(base, came, over, gains[1])
    over, up[3], down[3] = together(swap_chips(normed), up[3], down[3])
    up.append(shift(up[3][:256], z=1))
    down.append(shift(down[3][256:], z=-1))
    mlp = (*down[:4], up[4], up[3], up[2], up[1], down[4])
    base, away, over = mlp_call(place, first, (normed, shift(normed, c=1), over, shift(over, c=1)), mlp)
    came = shift(away, c=1)
    over = swap_chips((over + came[ROWS:]).astype(BF))
    second = (base + came[:ROWS] + over.astype(F32)).astype(BF)

    groups = [[(2 * m + core) * 8 + k for m in range(16) for k in range(8)] for core in range(2)]
    series = lax.all_to_all(second, AXES, split_axis=0, concat_axis=0, tiled=True, axis_index_groups=groups)
    base, away = time_call(place, series, shift(series, c=1), gains[2], shared)
    done = (base + shift(away, c=1)).astype(BF)
    return lax.all_to_all(done.reshape(1, ROWS, 1, width), "dp", split_axis=1, concat_axis=2, tiled=True)


def solution(mesh):
    return jax.shard_map(
        body,
        mesh=mesh,
        in_specs=(
            P(None, "dp", "fsdp", None),
            P(),
            P("fsdp", None),
            P("fsdp", None),
            P(),
            P("fsdp", None),
            P("fsdp", None),
            P(),
            P("fsdp", None),
            P("fsdp", None),
        ),
        out_specs=P(None, "dp", "fsdp", None),
        check_vma=False,
    )
```

```python
import functools

import jax
import jax.numpy as jnp
from jax import lax
from jax.experimental import pallas as pl
from jax.experimental.pallas import tpu as pltpu
from jax.sharding import PartitionSpec as P

BF = jnp.bfloat16
F32 = jnp.float32
AXES = ("dp", "fsdp")
ROWS = 128
HALF = 512
VMEM = pl.BlockSpec(memory_space=pltpu.VMEM)
SMEM = pl.BlockSpec(memory_space=pltpu.SMEM)
ANY = pl.BlockSpec(memory_space=pl.ANY)
BIG = pltpu.CompilerParams(vmem_limit_bytes=56 * 1024 * 1024)


def device(x, y, z, c):
    return (((z % 4) * 4 + y) * 2 + c) * 8 + (z // 4) * 4 + x


def chips():
    return [(x, y, z, c) for x in range(4) for y in range(4) for z in range(8) for c in range(2)]


def shift(v, x=0, y=0, z=0, c=0):
    pairs = [
        (device(a, b, d, e), device((a + x) % 4, (b + y) % 4, (d + z) % 8, (e + c) % 2)) for a, b, d, e in chips()
    ]
    return lax.ppermute(v, AXES, pairs)


def swap_chips(v):
    return lax.ppermute(v, AXES, [(device(a, b, d, e), device(a, b ^ 1, d, e)) for a, b, d, e in chips()])


def norm_rows(wide, gain):
    centre = jnp.mean(wide, axis=-1, keepdims=True)
    off = wide - centre
    spread = jnp.mean(off * off, axis=-1, keepdims=True)
    return (off * lax.rsqrt(spread + 1e-06) * gain).astype(BF)


def start_copies(pairs, sems):
    copies = []
    for i, (src, dst) in enumerate(pairs):
        copy = pltpu.make_async_copy(src, dst, sems.at[i])
        copy.start()
        copies.append(copy)
    return copies


def aligned(offset, size, unit):
    return pl.ds(pl.multiple_of(offset, unit), size)


def shares_kernel(place, sqkv, sproject, up, down, tqkv, tproject, near, reach,
                  sheads, srows, ups, downs, theads, trows, sems):
    y, c, zl, quarter = place[2], place[3], place[4], place[5]
    half = aligned(c * 64, 64, 64)
    pairs = [(sqkv, sheads), (sproject.at[half], srows)]
    for i in range(2):
        pairs.append((up.at[:, aligned((2 * zl + i) * 512 + quarter * 128, 128, 128)], ups.at[i]))
    pairs.append((down.at[aligned(quarter * 128 + zl * 32, 32, 32)], downs))
    for part in range(3):
        pairs.append((tqkv.at[:, aligned(part * 1024 + y * 256, 256, 256)], theads.at[part]))
    pairs.append((tproject.at[half, aligned(y * 256, 256, 256)], trows))
    for copy in start_copies(pairs, sems):
        copy.wait()

    source = lax.broadcasted_iota(jnp.int32, (512, 128), 0)
    lane = lax.broadcasted_iota(jnp.int32, (512, 128), 1)
    pick = (source == lane + jnp.where(lane < 64, 0, 192) + quarter * 64).astype(F32).astype(BF)
    for pair in range(2):
        at = pair * 128
        for part in range(3):
            block = sheads[:, part * 1024 + pair * 512 : part * 1024 + pair * 512 + 512]
            got = jnp.dot(block, pick, preferred_element_type=F32).astype(BF)
            for ref in (near, reach):
                ref[at : at + 128, part * 128 : part * 128 + 128] = got
        for ref in (near, reach):
            ref[at : at + 64, 384:512] = srows[:, pair * 256 : pair * 256 + 128]
            ref[at + 64 : at + 128, 384:512] = srows[:, pair * 256 + 128 : pair * 256 + 256]
    for ref in (near, reach):
        ref[256:320, :] = srows[:, 512:]
    for i in range(2):
        near[320:448, i * 128 : i * 128 + 128] = ups[i]
    for i in range(4):
        near[320 + i * 32 : 352 + i * 32, 256:512] = downs[:, i * 256 : i * 256 + 256]

    source = lax.broadcasted_iota(jnp.int32, (256, 128), 0)
    lane = lax.broadcasted_iota(jnp.int32, (256, 128), 1)
    pick = (source == lane + jnp.where(lane < 64, 0, 64) + c * 64).astype(F32).astype(BF)
    for part in range(3):
        reach[320:448, part * 128 : part * 128 + 128] = jnp.dot(theads[part], pick, preferred_element_type=F32).astype(BF)
    reach[320:384, 384:512] = trows[:, :128]
    reach[384:448, 384:512] = trows[:, 128:]


def make_shares(place, *weights):
    return pl.pallas_call(
        shares_kernel,
        out_shape=[jax.ShapeDtypeStruct((rows, HALF), BF) for rows in (448, 448)],
        in_specs=[SMEM] + [ANY] * 6,
        out_specs=[VMEM] * 2,
        scratch_shapes=[
            pltpu.VMEM((128, 3072), BF),
            pltpu.VMEM((64, 1024), BF),
            pltpu.VMEM((2, 128, 128), BF),
            pltpu.VMEM((32, 1024), BF),
            pltpu.VMEM((3, 128, 256), BF),
            pltpu.VMEM((64, 256), BF),
            pltpu.SemaphoreType.DMA((9,)),
        ],
        compiler_params=BIG,
        cost_estimate=pl.CostEstimate(flops=120000000, bytes_accessed=2500000, transcendentals=0),
    )(place, *weights)


def stack_kernel(a, b, c, d, out, sems):
    for copy in start_copies([(ref.at[pl.ds(320, 128)], out.at[pl.ds(i * 128, 128)]) for i, ref in enumerate((a, b, c, d))], sems):
        copy.wait()


def stack(pieces):
    return pl.pallas_call(
        stack_kernel,
        out_shape=jax.ShapeDtypeStruct((512, HALF), BF),
        in_specs=[ANY] * 4,
        out_specs=VMEM,
        scratch_shapes=[pltpu.SemaphoreType.DMA((4,))],
        compiler_params=BIG,
        cost_estimate=pl.CostEstimate(flops=0, bytes_accessed=1000000, transcendentals=0),
    )(*pieces)


def attend_pair(query, keys, values, seqs):
    count = query.shape[0]
    low = lax.broadcasted_iota(jnp.int32, (count, 128), 1) < 64
    mixed = []
    for mask in (low, jnp.logical_not(low)):
        one = jnp.where(mask, query, jnp.zeros_like(query))
        scores = lax.dot_general(one, keys, (((1,), (1,)), ((), ())), preferred_element_type=F32)
        if seqs > 1:
            length = count // seqs
            row = lax.broadcasted_iota(jnp.int32, (count, count), 0) // length
            column = lax.broadcasted_iota(jnp.int32, (count, count), 1) // length
            scores = jnp.where(row == column, scores, -1e30)
        weights = jnp.exp(scores - jnp.max(scores, axis=-1, keepdims=True))
        total = jnp.sum(weights, axis=-1, keepdims=True)
        mixed.append(jnp.dot(weights.astype(BF), values, preferred_element_type=F32) * (1.0 / total))
    return jnp.where(low, mixed[0], mixed[1]).astype(BF)


def space_kernel(place, own, other, far, far_other, gain, *refs):
    pieces = refs[:8]
    base, away, over, tokens, wqkv, wout, packed, att, sems = refs[8:]
    blocks = [
        (lax.rem(place[1] + step // 4, 2) * 4 + lax.rem(place[0] + step, 4), ref) for step, ref in enumerate(pieces)
    ]
    pairs = []
    for pair in range(2):
        for block, ref in blocks:
            pairs.append((ref.at[pl.ds(pair * 128, 128), pl.ds(0, 384)],
                          wqkv.at[aligned(block * 128, 128, 128), pl.ds(pair * 384, 384)]))
    copies = start_copies(pairs, sems)
    odd = lax.rem(place[0] + place[2], 2)
    late = []
    for slot in range(4):
        ways = []
        for parity in range(2):
            block, ref = blocks[(slot // 2) * 4 + (slot % 2) * 2 + parity]
            row = aligned(lax.div(block, 2) * 64, 64, 64)
            ways.append([
                pltpu.make_async_copy(src, wout.at[row, pl.ds(column, src.shape[1])], sems.at[16 + slot * 5 + i])
                for i, (src, column) in enumerate(
                    [(ref.at[pl.ds(256, 64), :], 512)]
                    + [(ref.at[pl.ds(k * 64, 64), pl.ds(384, 128)], k * 128) for k in range(4)])
            ])
        for parity in range(2):

            @pl.when(odd == parity)
            def _():
                for copy in ways[parity]:
                    copy.start()

        late.append(ways)
    for i, ref in enumerate((own, other, far, far_other)):
        tokens[i * ROWS : (i + 1) * ROWS, :] = norm_rows(ref[...].astype(F32), gain[...])
    for pair in range(2):
        for copy in copies[pair * 8 : pair * 8 + 8]:
            copy.wait()
        cols = slice(pair * 384, pair * 384 + 384)
        packed[:, cols] = jnp.dot(tokens[...], wqkv[:, cols], preferred_element_type=F32).astype(BF)
        for frame in range(2):
            rows = slice(frame * 256, frame * 256 + 256)
            query, keys, values = (packed[rows, pair * 384 + i * 128 : pair * 384 + i * 128 + 128] for i in range(3))
            att[rows, pair * 128 : pair * 128 + 128] = attend_pair(query * 0.125, keys, values, 1)
    for ways in late:
        for parity in range(2):

            @pl.when(odd == parity)
            def _():
                for copy in ways[parity]:
                    copy.wait()

    row = lambda i: jnp.dot(att[i * ROWS : (i + 1) * ROWS, :], wout[...], preferred_element_type=F32)
    away[:ROWS, :] = row(1).astype(BF)
    away[ROWS:, :] = row(3).astype(BF)
    over[...] = row(2)
    base[...] = own[...].astype(F32) + row(0)


def wide(rows, dtype=F32):
    return jax.ShapeDtypeStruct((rows, 1024), dtype)


def space_call(place, tokens, gain, pieces):
    return pl.pallas_call(
        space_kernel,
        out_shape=[wide(ROWS), wide(2 * ROWS, BF), wide(ROWS)],
        in_specs=[SMEM] + [VMEM] * 5 + [ANY] * 8,
        out_specs=[VMEM] * 3,
        scratch_shapes=[
            pltpu.VMEM((4 * ROWS, 1024), BF),
            pltpu.VMEM((1024, 768), BF),
            pltpu.VMEM((256, 1024), BF),
            pltpu.VMEM((4 * ROWS, 768), BF),
            pltpu.VMEM((4 * ROWS, 256), BF),
            pltpu.SemaphoreType.DMA((36,)),
        ],
        compiler_params=BIG,
        cost_estimate=pl.CostEstimate(flops=1400000000, bytes_accessed=6000000, transcendentals=600000),
    )(place, *tokens, gain, *pieces)


def norm_kernel(base, came, over, gain, first, normed):
    summed = (base[...] + came[:ROWS, :].astype(F32) + over[...].astype(F32)).astype(BF)
    first[...] = summed
    normed[...] = norm_rows(summed.astype(F32), gain[...])


def norm_call(base, came, over, gain):
    return pl.pallas_call(
        norm_kernel,
        out_shape=[jax.ShapeDtypeStruct((ROWS, 1024), BF)] * 2,
        in_specs=[VMEM] * 4,
        out_specs=[VMEM] * 2,
        cost_estimate=pl.CostEstimate(flops=2000000, bytes_accessed=2500000, transcendentals=0),
    )(base, came, over, gain)


def mlp_kernel(place, first, own, other, far, far_other, *refs):
    pieces, refs = refs[:9], refs[9:]
    base, away, over, tokens, wup, wdown, hidden, sems = refs
    pairs, lower = [], []
    for step in range(8):
        z = lax.rem(place[1] * 4 + place[4] + step, 8)
        zl = lax.rem(z, 4)
        for rx in range(4):
            ref, at = pieces[step], rx * 128
            if step == 4:
                ref, at = pieces[4 + rx // 2 * 4], rx % 2 * 128
            block = lax.div(z, 4) * 4 + lax.rem(place[0] + rx, 4)
            pairs.append((ref.at[pl.ds(at, 128), pl.ds(0, 256)],
                          wup.at[aligned(block * 128, 128, 128), aligned(zl * 256, 256, 256)]))
            lower.append((ref.at[pl.ds(at, 128), pl.ds(256, 256)], wdown.at[block * 4 + zl]))
    copies = start_copies(pairs + lower, sems)
    for i, ref in enumerate((own, other, far, far_other)):
        tokens[i * ROWS : (i + 1) * ROWS, :] = ref[...]
    for copy in copies[: len(pairs)]:
        copy.wait()
    for part in range(2):
        cols = slice(part * HALF, (part + 1) * HALF)
        inner = jnp.dot(tokens[...], wup[:, cols], preferred_element_type=F32)
        hidden[:, cols] = jax.nn.gelu(inner, approximate=True).astype(BF)
    for copy in copies[len(pairs) :]:
        copy.wait()
    for part in range(4):
        cols = slice(part * 256, part * 256 + 256)
        got = jnp.dot(hidden[...], wdown[:, part * 32 : part * 32 + 32, :].reshape(1024, 256), preferred_element_type=F32)
        base[:, cols] = first[:, cols].astype(F32) + got[:ROWS]
        away[:ROWS, cols] = got[ROWS : 2 * ROWS].astype(BF)
        over[:, cols] = got[2 * ROWS : 3 * ROWS]
        away[ROWS:, cols] = got[3 * ROWS :].astype(BF)


def mlp_call(place, first, tokens, pieces):
    return pl.pallas_call(
        mlp_kernel,
        out_shape=[wide(ROWS), wide(2 * ROWS, BF), wide(ROWS)],
        in_specs=[SMEM] + [VMEM] * 5 + [ANY] * 9,
        out_specs=[VMEM] * 3,
        scratch_shapes=[
            pltpu.VMEM((4 * ROWS, 1024), BF),
            pltpu.VMEM((1024, 1024), BF),
            pltpu.VMEM((32, 128, 256), BF),
            pltpu.VMEM((4 * ROWS, 1024), BF),
            pltpu.SemaphoreType.DMA((64,)),
        ],
        compiler_params=BIG,
        cost_estimate=pl.CostEstimate(flops=2200000000, bytes_accessed=9000000, transcendentals=600000),
    )(place, first, *tokens, *pieces)


def time_kernel(place, own, other, gain, shared, base, away, tokens, weights, packed, att, sems):
    pairs = []
    for y in range(4):
        for x in range(4):
            for rz in range(2):
                block = lax.rem(place[1] + rz, 2) * 4 + x
                pairs.append((shared.at[pl.ds(((y * 4 + x) * 2 + rz) * 128, 128)],
                              weights.at[aligned(block * 128, 128, 128), pl.ds(y * HALF, HALF)]))
    copies = start_copies(pairs, sems)
    tokens[:ROWS, :] = norm_rows(own[...].astype(F32), gain[...])
    tokens[ROWS:, :] = norm_rows(other[...].astype(F32), gain[...])
    for pair in range(4):
        for copy in copies[pair * 8 : pair * 8 + 8]:
            copy.wait()
        at = pair * 384
        packed[:, at : at + 384] = jnp.dot(
            tokens[...], weights[:, pair * HALF : pair * HALF + 384], preferred_element_type=F32).astype(BF)
        query, keys, values = (packed[:, at + i * 128 : at + i * 128 + 128] for i in range(3))
        att[:, pair * 128 : pair * 128 + 128] = attend_pair(query * 0.125, keys, values, 2)
    for pair in range(4):
        lanes = slice(pair * HALF + 384, pair * HALF + 512)
        rows = jnp.concatenate([
            jnp.concatenate([weights[block * 128 + i * 64 : block * 128 + i * 64 + 64, lanes] for block in range(8)], axis=0)
            for i in range(2)], axis=1)
        cols = slice(pair * 256, pair * 256 + 256)
        got = jnp.dot(att[...], rows, preferred_element_type=F32)
        base[:, cols] = own[:, cols].astype(F32) + got[:ROWS]
        away[:, cols] = got[ROWS:].astype(BF)


def time_call(place, own, other, gain, shared):
    return pl.pallas_call(
        time_kernel,
        out_shape=[wide(ROWS), wide(ROWS, BF)],
        in_specs=[SMEM] + [VMEM] * 3 + [ANY],
        out_specs=[VMEM] * 2,
        scratch_shapes=[
            pltpu.VMEM((2 * ROWS, 1024), BF),
            pltpu.VMEM((1024, 2048), BF),
            pltpu.VMEM((2 * ROWS, 1536), BF),
            pltpu.VMEM((2 * ROWS, 512), BF),
            pltpu.SemaphoreType.DMA((32,)),
        ],
        compiler_params=pltpu.CompilerParams(vmem_limit_bytes=24 * 1024 * 1024),
        cost_estimate=pl.CostEstimate(flops=1400000000, bytes_accessed=6000000, transcendentals=600000),
    )(place, own, other, gain, shared)


def leave_kernel(base, came, out):
    done = base[...] + came[...].astype(F32)
    left, right = done[:, :HALF].reshape(16, 8, HALF), done[:, HALF:].reshape(16, 8, HALF)
    upper = lax.broadcasted_iota(jnp.int32, (16, 8, HALF), 1) < 4
    turn = lambda v: jnp.concatenate([v[:, 4:], v[:, :4]], axis=1)
    out[:, 0] = jnp.where(upper, left, turn(right)).astype(BF)
    out[:, 1] = jnp.where(upper, turn(left), right).astype(BF)


def leave_call(base, came):
    return pl.pallas_call(
        leave_kernel,
        out_shape=jax.ShapeDtypeStruct((16, 2, 8, HALF), BF),
        in_specs=[VMEM] * 2,
        out_specs=VMEM,
        cost_estimate=pl.CostEstimate(flops=1000000, bytes_accessed=1300000, transcendentals=0),
    )(base, came).reshape(32, 8, HALF)


def arrive_kernel(came, out):
    wide_rows = came[...].astype(F32)
    for frame in range(4):
        for half in range(2):
            out[0, frame, :, half * HALF : half * HALF + HALF] = wide_rows[:, half * 4 + frame, :].astype(BF)


def arrive_call(came):
    return pl.pallas_call(
        arrive_kernel,
        out_shape=jax.ShapeDtypeStruct((1, 4, 32, 1024), BF),
        in_specs=[VMEM],
        out_specs=VMEM,
        cost_estimate=pl.CostEstimate(flops=1000000, bytes_accessed=500000, transcendentals=0),
    )(came)


def body(clip, space_gain, space_qkv, space_out, mlp_gain, mlp_up, mlp_down, time_gain, time_qkv, time_out):
    dp, fs = lax.axis_index("dp"), lax.axis_index("fsdp")
    x, zh, c, y, zl = lax.rem(fs, 4), lax.div(fs, 4), lax.rem(dp, 2), lax.rem(lax.div(dp, 2), 4), lax.div(dp, 8)
    place = jnp.stack([x, zh, y, c, zl, lax.rem(y, 2) * 2 + c]).astype(jnp.int32)
    width = clip.shape[-1]
    gains = [gain.reshape(1, width) for gain in (space_gain, mlp_gain, time_gain)]

    together = lambda *v: lax.optimization_barrier(v)
    planes = [[device(px, py, z, core) for py in range(4) for px in range(4)] for z in range(8) for core in range(2)]
    near, reach = make_shares(place, space_qkv, space_out, mlp_up, mlp_down, time_qkv, time_out)
    far = shift(reach, z=4)
    near = near, shift(near, x=-1), shift(near, x=2), shift(near, x=1)
    split = clip.reshape(4, 16, 2, width)
    keep = jnp.where(c == 0, split[:, :, 0], split[:, :, 1])
    give = jnp.where(c == 0, split[:, :, 1], split[:, :, 0])
    taken = shift(give, c=1)
    frames = jnp.where(c == 0, jnp.concatenate([keep, taken], axis=0), jnp.concatenate([taken, keep], axis=0))
    frames = lax.all_to_all(frames, "fsdp", split_axis=0, concat_axis=0, tiled=True)
    own = frames.transpose(1, 0, 2).reshape(ROWS, width)
    far, *near = together(far, *near)
    piece = far[:320]
    far = far, shift(piece, x=-1), shift(piece, x=2), shift(piece, x=1)
    mlp = stack(near)
    over = swap_chips(own)
    up, down = [mlp, shift(mlp, z=1)], [mlp, shift(mlp, z=-1)]
    over, up[1], down[1], *far = together(over, up[1], down[1], *far)
    up.append(shift(up[1], z=1))
    down.append(shift(down[1], z=-1))
    space = (*near, *far)
    shared = jnp.concatenate([reach[320:], far[0][320:]], axis=0)
    shared = lax.all_gather(shared, AXES, axis=0, tiled=True, axis_index_groups=planes)

    base, away, over = space_call(place, (own, shift(own, c=1), over, shift(over, c=1)), gains[0], space)
    away, up[2], down[2] = together(away, up[2], down[2])
    up.append(shift(up[2], z=1))
    down.append(shift(down[2], z=-1))
    came = shift(away, c=1)
    over = swap_chips((over + came[ROWS:]).astype(BF))
    over, up[3], down[3] = together(over, up[3], down[3])
    up.append(shift(up[3][:256], z=1))
    down.append(shift(down[3][256:], z=-1))
    first, normed = norm_call(base, came, over, gains[1])
    over = swap_chips(normed)
    mlp = (*down[:4], up[4], up[3], up[2], up[1], down[4])
    base, away, over = mlp_call(place, first, (normed, shift(normed, c=1), over, shift(over, c=1)), mlp)
    came = shift(away, c=1)
    over = swap_chips((over + came[ROWS:]).astype(BF))
    second = (base + came[:ROWS] + over.astype(F32)).astype(BF)

    groups = [[(2 * m + core) * 8 + k for m in range(16) for k in range(8)] for core in range(2)]
    series = lax.all_to_all(second, AXES, split_axis=0, concat_axis=0, tiled=True, axis_index_groups=groups)
    base, away = time_call(place, series, shift(series, c=1), gains[2], shared)
    done = leave_call(base, shift(away, c=1))
    return arrive_call(lax.all_to_all(done, "dp", split_axis=0, concat_axis=0, tiled=True))


def solution(mesh):
    return jax.shard_map(
        body,
        mesh=mesh,
        in_specs=(
            P(None, "dp", "fsdp", None),
            P(),
            P("fsdp", None),
            P("fsdp", None),
            P(),
            P("fsdp", None),
            P("fsdp", None),
            P(),
            P("fsdp", None),
            P("fsdp", None),
        ),
        out_specs=P(None, "dp", "fsdp", None),
        check_vma=False,
    )
```

```python
import functools

import jax
import jax.numpy as jnp
from jax import lax
from jax.experimental import pallas as pl
from jax.experimental.pallas import tpu as pltpu
from jax.sharding import PartitionSpec as P

BF = jnp.bfloat16
F32 = jnp.float32
AXES = ("dp", "fsdp")
ROWS = 128
HALF = 512
VMEM = pl.BlockSpec(memory_space=pltpu.VMEM)
SMEM = pl.BlockSpec(memory_space=pltpu.SMEM)
ANY = pl.BlockSpec(memory_space=pl.ANY)
BIG = pltpu.CompilerParams(vmem_limit_bytes=56 * 1024 * 1024)


def device(x, y, z, c):
    return (((z % 4) * 4 + y) * 2 + c) * 8 + (z // 4) * 4 + x


def chips():
    return [(x, y, z, c) for x in range(4) for y in range(4) for z in range(8) for c in range(2)]


def shift(v, x=0, y=0, z=0, c=0):
    pairs = [
        (device(a, b, d, e), device((a + x) % 4, (b + y) % 4, (d + z) % 8, (e + c) % 2)) for a, b, d, e in chips()
    ]
    return lax.ppermute(v, AXES, pairs)


def swap_chips(v):
    return lax.ppermute(v, AXES, [(device(a, b, d, e), device(a, b ^ 1, d, e)) for a, b, d, e in chips()])


def norm_rows(wide, gain):
    centre = jnp.mean(wide, axis=-1, keepdims=True)
    off = wide - centre
    spread = jnp.mean(off * off, axis=-1, keepdims=True)
    return (off * lax.rsqrt(spread + 1e-06) * gain).astype(BF)


def start_copies(pairs, sems):
    copies = []
    for i, (src, dst) in enumerate(pairs):
        copy = pltpu.make_async_copy(src, dst, sems.at[i])
        copy.start()
        copies.append(copy)
    return copies


def aligned(offset, size, unit):
    return pl.ds(pl.multiple_of(offset, unit), size)


def shares_kernel(place, sqkv, sproject, up, down, tqkv, tproject, near, reach,
                  sheads, srows, ups, downs, theads, trows, sems):
    y, c, zl, quarter = place[2], place[3], place[4], place[5]
    half = aligned(c * 64, 64, 64)
    pairs = [(sproject.at[half], srows)]
    for part in range(3):
        for j in range(4):
            column = part * 1024 + j * 256 + lax.div(quarter, 2) * 128
            pairs.append((sqkv.at[:, aligned(column, 128, 128)], sheads.at[:, pl.ds((part * 4 + j) * 128, 128)]))
    for i in range(2):
        pairs.append((up.at[:, aligned((2 * zl + i) * 512 + quarter * 128, 128, 128)], ups.at[i]))
    pairs.append((down.at[aligned(quarter * 128 + zl * 32, 32, 32)], downs))
    for part in range(3):
        pairs.append((tqkv.at[:, aligned(part * 1024 + y * 256, 256, 256)], theads.at[part]))
    pairs.append((tproject.at[half, aligned(y * 256, 256, 256)], trows))
    for copy in start_copies(pairs, sems):
        copy.wait()

    source = lax.broadcasted_iota(jnp.int32, (256, 128), 0)
    lane = lax.broadcasted_iota(jnp.int32, (256, 128), 1)
    pick = (source == lane + jnp.where(lane < 64, 0, 64) + c * 64).astype(F32).astype(BF)
    for pair in range(2):
        at = pair * 128
        for part in range(3):
            block = sheads[:, part * 512 + pair * 256 : part * 512 + pair * 256 + 256]
            got = jnp.dot(block, pick, preferred_element_type=F32).astype(BF)
            for ref in (near, reach):
                ref[at : at + 128, part * 128 : part * 128 + 128] = got
        for ref in (near, reach):
            ref[at : at + 64, 384:512] = srows[:, pair * 256 : pair * 256 + 128]
            ref[at + 64 : at + 128, 384:512] = srows[:, pair * 256 + 128 : pair * 256 + 256]
    for ref in (near, reach):
        ref[256:320, :] = srows[:, 512:]
    for i in range(2):
        near[320:448, i * 128 : i * 128 + 128] = ups[i]
    for i in range(4):
        near[320 + i * 32 : 352 + i * 32, 256:512] = downs[:, i * 256 : i * 256 + 256]

    for part in range(3):
        reach[320:448, part * 128 : part * 128 + 128] = jnp.dot(theads[part], pick, preferred_element_type=F32).astype(BF)
    reach[320:384, 384:512] = trows[:, :128]
    reach[384:448, 384:512] = trows[:, 128:]


def make_shares(place, *weights):
    return pl.pallas_call(
        shares_kernel,
        out_shape=[jax.ShapeDtypeStruct((rows, HALF), BF) for rows in (448, 448)],
        in_specs=[SMEM] + [ANY] * 6,
        out_specs=[VMEM] * 2,
        scratch_shapes=[
            pltpu.VMEM((128, 1536), BF),
            pltpu.VMEM((64, 1024), BF),
            pltpu.VMEM((2, 128, 128), BF),
            pltpu.VMEM((32, 1024), BF),
            pltpu.VMEM((3, 128, 256), BF),
            pltpu.VMEM((64, 256), BF),
            pltpu.SemaphoreType.DMA((20,)),
        ],
        compiler_params=BIG,
        cost_estimate=pl.CostEstimate(flops=120000000, bytes_accessed=2500000, transcendentals=0),
    )(place, *weights)


def stack_kernel(a, b, c, d, out, sems):
    for copy in start_copies([(ref.at[pl.ds(320, 128)], out.at[pl.ds(i * 128, 128)]) for i, ref in enumerate((a, b, c, d))], sems):
        copy.wait()


def stack(pieces):
    return pl.pallas_call(
        stack_kernel,
        out_shape=jax.ShapeDtypeStruct((512, HALF), BF),
        in_specs=[ANY] * 4,
        out_specs=VMEM,
        scratch_shapes=[pltpu.SemaphoreType.DMA((4,))],
        compiler_params=BIG,
        cost_estimate=pl.CostEstimate(flops=0, bytes_accessed=1000000, transcendentals=0),
    )(*pieces)


def attend_pair(query, keys, values, seqs):
    count = query.shape[0]
    low = lax.broadcasted_iota(jnp.int32, (count, 128), 1) < 64
    mixed = []
    for mask in (low, jnp.logical_not(low)):
        one = jnp.where(mask, query, jnp.zeros_like(query))
        scores = lax.dot_general(one, keys, (((1,), (1,)), ((), ())), preferred_element_type=F32)
        if seqs > 1:
            length = count // seqs
            row = lax.broadcasted_iota(jnp.int32, (count, count), 0) // length
            column = lax.broadcasted_iota(jnp.int32, (count, count), 1) // length
            scores = jnp.where(row == column, scores, -1e30)
        weights = jnp.exp(scores - jnp.max(scores, axis=-1, keepdims=True))
        total = jnp.sum(weights, axis=-1, keepdims=True)
        mixed.append(jnp.dot(weights.astype(BF), values, preferred_element_type=F32) * (1.0 / total))
    return jnp.where(low, mixed[0], mixed[1]).astype(BF)


def space_kernel(place, own, other, far, far_other, gain, *refs):
    pieces = refs[:8]
    base, away, over, tokens, wqkv, wout, packed, att, sems = refs[8:]
    blocks = [
        (lax.rem(place[1] + step // 4, 2) * 4 + lax.rem(place[0] + step, 4), ref) for step, ref in enumerate(pieces)
    ]
    pairs = []
    for pair in range(2):
        for block, ref in blocks:
            pairs.append((ref.at[pl.ds(pair * 128, 128), pl.ds(0, 384)],
                          wqkv.at[aligned(block * 128, 128, 128), pl.ds(pair * 384, 384)]))
    copies = start_copies(pairs, sems)
    odd = lax.rem(place[0] + place[2], 2)
    late = []
    for slot in range(4):
        ways = []
        for parity in range(2):
            block, ref = blocks[(slot // 2) * 4 + (slot % 2) * 2 + parity]
            row = aligned(lax.div(block, 2) * 64, 64, 64)
            ways.append([
                pltpu.make_async_copy(src, wout.at[row, pl.ds(column, src.shape[1])], sems.at[16 + slot * 5 + i])
                for i, (src, column) in enumerate(
                    [(ref.at[pl.ds(256, 64), :], 512)]
                    + [(ref.at[pl.ds(k * 64, 64), pl.ds(384, 128)], k * 128) for k in range(4)])
            ])
        for parity in range(2):

            @pl.when(odd == parity)
            def _():
                for copy in ways[parity]:
                    copy.start()

        late.append(ways)
    for i, ref in enumerate((own, other, far, far_other)):
        tokens[i * ROWS : (i + 1) * ROWS, :] = norm_rows(ref[...].astype(F32), gain[...])
    for pair in range(2):
        for copy in copies[pair * 8 : pair * 8 + 8]:
            copy.wait()
        cols = slice(pair * 384, pair * 384 + 384)
        packed[:, cols] = jnp.dot(tokens[...], wqkv[:, cols], preferred_element_type=F32).astype(BF)
        for frame in range(2):
            rows = slice(frame * 256, frame * 256 + 256)
            query, keys, values = (packed[rows, pair * 384 + i * 128 : pair * 384 + i * 128 + 128] for i in range(3))
            att[rows, pair * 128 : pair * 128 + 128] = attend_pair(query * 0.125, keys, values, 1)
    for ways in late:
        for parity in range(2):

            @pl.when(odd == parity)
            def _():
                for copy in ways[parity]:
                    copy.wait()

    row = lambda i: jnp.dot(att[i * ROWS : (i + 1) * ROWS, :], wout[...], preferred_element_type=F32)
    away[:ROWS, :] = row(1).astype(BF)
    away[ROWS:, :] = row(3).astype(BF)
    over[...] = row(2)
    base[...] = own[...].astype(F32) + row(0)


def wide(rows, dtype=F32):
    return jax.ShapeDtypeStruct((rows, 1024), dtype)


def space_call(place, tokens, gain, pieces):
    return pl.pallas_call(
        space_kernel,
        out_shape=[wide(ROWS), wide(2 * ROWS, BF), wide(ROWS)],
        in_specs=[SMEM] + [VMEM] * 5 + [ANY] * 8,
        out_specs=[VMEM] * 3,
        scratch_shapes=[
            pltpu.VMEM((4 * ROWS, 1024), BF),
            pltpu.VMEM((1024, 768), BF),
            pltpu.VMEM((256, 1024), BF),
            pltpu.VMEM((4 * ROWS, 768), BF),
            pltpu.VMEM((4 * ROWS, 256), BF),
            pltpu.SemaphoreType.DMA((36,)),
        ],
        compiler_params=BIG,
        cost_estimate=pl.CostEstimate(flops=1400000000, bytes_accessed=6000000, transcendentals=600000),
    )(place, *tokens, gain, *pieces)


def norm_kernel(base, came, over, gain, first, normed):
    summed = (base[...] + came[:ROWS, :].astype(F32) + over[...].astype(F32)).astype(BF)
    first[...] = summed
    normed[...] = norm_rows(summed.astype(F32), gain[...])


def norm_call(base, came, over, gain):
    return pl.pallas_call(
        norm_kernel,
        out_shape=[jax.ShapeDtypeStruct((ROWS, 1024), BF)] * 2,
        in_specs=[VMEM] * 4,
        out_specs=[VMEM] * 2,
        cost_estimate=pl.CostEstimate(flops=2000000, bytes_accessed=2500000, transcendentals=0),
    )(base, came, over, gain)


def mlp_kernel(place, first, own, other, far, far_other, *refs):
    pieces, refs = refs[:9], refs[9:]
    base, away, over, tokens, wup, wdown, hidden, sems = refs
    pairs, lower = [], []
    for step in range(8):
        z = lax.rem(place[1] * 4 + place[4] + step, 8)
        zl = lax.rem(z, 4)
        for rx in range(4):
            ref, at = pieces[step], rx * 128
            if step == 4:
                ref, at = pieces[4 + rx // 2 * 4], rx % 2 * 128
            block = lax.div(z, 4) * 4 + lax.rem(place[0] + rx, 4)
            pairs.append((ref.at[pl.ds(at, 128), pl.ds(0, 256)],
                          wup.at[aligned(block * 128, 128, 128), aligned(zl * 256, 256, 256)]))
            lower.append((ref.at[pl.ds(at, 128), pl.ds(256, 256)], wdown.at[block * 4 + zl]))
    copies = start_copies(pairs + lower, sems)
    for i, ref in enumerate((own, other, far, far_other)):
        tokens[i * ROWS : (i + 1) * ROWS, :] = ref[...]
    for copy in copies[: len(pairs)]:
        copy.wait()
    for part in range(2):
        cols = slice(part * HALF, (part + 1) * HALF)
        inner = jnp.dot(tokens[...], wup[:, cols], preferred_element_type=F32)
        hidden[:, cols] = jax.nn.gelu(inner, approximate=True).astype(BF)
    for copy in copies[len(pairs) :]:
        copy.wait()
    for part in range(4):
        cols = slice(part * 256, part * 256 + 256)
        got = jnp.dot(hidden[...], wdown[:, part * 32 : part * 32 + 32, :].reshape(1024, 256), preferred_element_type=F32)
        base[:, cols] = first[:, cols].astype(F32) + got[:ROWS]
        away[:ROWS, cols] = got[ROWS : 2 * ROWS].astype(BF)
        over[:, cols] = got[2 * ROWS : 3 * ROWS]
        away[ROWS:, cols] = got[3 * ROWS :].astype(BF)


def mlp_call(place, first, tokens, pieces):
    return pl.pallas_call(
        mlp_kernel,
        out_shape=[wide(ROWS), wide(2 * ROWS, BF), wide(ROWS)],
        in_specs=[SMEM] + [VMEM] * 5 + [ANY] * 9,
        out_specs=[VMEM] * 3,
        scratch_shapes=[
            pltpu.VMEM((4 * ROWS, 1024), BF),
            pltpu.VMEM((1024, 1024), BF),
            pltpu.VMEM((32, 128, 256), BF),
            pltpu.VMEM((4 * ROWS, 1024), BF),
            pltpu.SemaphoreType.DMA((64,)),
        ],
        compiler_params=BIG,
        cost_estimate=pl.CostEstimate(flops=2200000000, bytes_accessed=9000000, transcendentals=600000),
    )(place, first, *tokens, *pieces)


def time_kernel(place, own, other, gain, shared, base, away, tokens, weights, packed, att, sems):
    pairs = []
    for y in range(4):
        for x in range(4):
            for rz in range(2):
                block = lax.rem(place[1] + rz, 2) * 4 + x
                pairs.append((shared.at[pl.ds(((y * 4 + x) * 2 + rz) * 128, 128)],
                              weights.at[aligned(block * 128, 128, 128), pl.ds(y * HALF, HALF)]))
    copies = start_copies(pairs, sems)
    tokens[:ROWS, :] = norm_rows(own[...].astype(F32), gain[...])
    tokens[ROWS:, :] = norm_rows(other[...].astype(F32), gain[...])
    for pair in range(4):
        for copy in copies[pair * 8 : pair * 8 + 8]:
            copy.wait()
        at = pair * 384
        packed[:, at : at + 384] = jnp.dot(
            tokens[...], weights[:, pair * HALF : pair * HALF + 384], preferred_element_type=F32).astype(BF)
        query, keys, values = (packed[:, at + i * 128 : at + i * 128 + 128] for i in range(3))
        att[:, pair * 128 : pair * 128 + 128] = attend_pair(query * 0.125, keys, values, 2)
    for pair in range(4):
        lanes = slice(pair * HALF + 384, pair * HALF + 512)
        rows = jnp.concatenate([
            jnp.concatenate([weights[block * 128 + i * 64 : block * 128 + i * 64 + 64, lanes] for block in range(8)], axis=0)
            for i in range(2)], axis=1)
        cols = slice(pair * 256, pair * 256 + 256)
        got = jnp.dot(att[...], rows, preferred_element_type=F32)
        base[:, cols] = own[:, cols].astype(F32) + got[:ROWS]
        away[:, cols] = got[ROWS:].astype(BF)


def time_call(place, own, other, gain, shared):
    return pl.pallas_call(
        time_kernel,
        out_shape=[wide(ROWS), wide(ROWS, BF)],
        in_specs=[SMEM] + [VMEM] * 3 + [ANY],
        out_specs=[VMEM] * 2,
        scratch_shapes=[
            pltpu.VMEM((2 * ROWS, 1024), BF),
            pltpu.VMEM((1024, 2048), BF),
            pltpu.VMEM((2 * ROWS, 1536), BF),
            pltpu.VMEM((2 * ROWS, 512), BF),
            pltpu.SemaphoreType.DMA((32,)),
        ],
        compiler_params=pltpu.CompilerParams(vmem_limit_bytes=24 * 1024 * 1024),
        cost_estimate=pl.CostEstimate(flops=1400000000, bytes_accessed=6000000, transcendentals=600000),
    )(place, own, other, gain, shared)


def leave_kernel(base, came, out):
    done = base[...] + came[...].astype(F32)
    left, right = done[:, :HALF].reshape(16, 8, HALF), done[:, HALF:].reshape(16, 8, HALF)
    upper = lax.broadcasted_iota(jnp.int32, (16, 8, HALF), 1) < 4
    turn = lambda v: jnp.concatenate([v[:, 4:], v[:, :4]], axis=1)
    out[:, 0] = jnp.where(upper, left, turn(right)).astype(BF)
    out[:, 1] = jnp.where(upper, turn(left), right).astype(BF)


def leave_call(base, came):
    return pl.pallas_call(
        leave_kernel,
        out_shape=jax.ShapeDtypeStruct((16, 2, 8, HALF), BF),
        in_specs=[VMEM] * 2,
        out_specs=VMEM,
        cost_estimate=pl.CostEstimate(flops=1000000, bytes_accessed=1300000, transcendentals=0),
    )(base, came).reshape(32, 8, HALF)


def arrive_kernel(came, out):
    wide_rows = came[...].astype(F32)
    for frame in range(4):
        for half in range(2):
            out[0, frame, :, half * HALF : half * HALF + HALF] = wide_rows[:, half * 4 + frame, :].astype(BF)


def arrive_call(came):
    return pl.pallas_call(
        arrive_kernel,
        out_shape=jax.ShapeDtypeStruct((1, 4, 32, 1024), BF),
        in_specs=[VMEM],
        out_specs=VMEM,
        cost_estimate=pl.CostEstimate(flops=1000000, bytes_accessed=500000, transcendentals=0),
    )(came)


def body(clip, space_gain, space_qkv, space_out, mlp_gain, mlp_up, mlp_down, time_gain, time_qkv, time_out):
    dp, fs = lax.axis_index("dp"), lax.axis_index("fsdp")
    x, zh, c, y, zl = lax.rem(fs, 4), lax.div(fs, 4), lax.rem(dp, 2), lax.rem(lax.div(dp, 2), 4), lax.div(dp, 8)
    place = jnp.stack([x, zh, y, c, zl, lax.rem(y, 2) * 2 + c]).astype(jnp.int32)
    width = clip.shape[-1]
    gains = [gain.reshape(1, width) for gain in (space_gain, mlp_gain, time_gain)]

    together = lambda *v: lax.optimization_barrier(v)
    planes = [[device(px, py, z, core) for py in range(4) for px in range(4)] for z in range(8) for core in range(2)]
    near, reach = make_shares(place, space_qkv, space_out, mlp_up, mlp_down, time_qkv, time_out)
    far = shift(reach, z=4)
    near = near, shift(near, x=-1), shift(near, x=2), shift(near, x=1)
    split = clip.reshape(4, 16, 2, width)
    keep = jnp.where(c == 0, split[:, :, 0], split[:, :, 1])
    give = jnp.where(c == 0, split[:, :, 1], split[:, :, 0])
    taken = shift(give, c=1)
    frames = jnp.where(c == 0, jnp.concatenate([keep, taken], axis=0), jnp.concatenate([taken, keep], axis=0))
    frames = lax.all_to_all(frames, "fsdp", split_axis=0, concat_axis=0, tiled=True)
    own = frames.transpose(1, 0, 2).reshape(ROWS, width)
    far, *near = together(far, *near)
    piece = far[:320]
    far_right = shift(piece, x=-1)
    far = far, far_right, shift(far_right, x=-1), shift(piece, x=1)
    mlp = stack(near)
    over = swap_chips(own)
    up, down = [mlp, shift(mlp, z=1)], [mlp, shift(mlp, z=-1)]
    over, up[1], down[1], *far = together(over, up[1], down[1], *far)
    up.append(shift(up[1], z=1))
    down.append(shift(down[1], z=-1))
    space = (*near, *far)
    shared = jnp.concatenate([reach[320:], far[0][320:]], axis=0)
    shared = lax.all_gather(shared, AXES, axis=0, tiled=True, axis_index_groups=planes)

    base, away, over = space_call(place, (own, shift(own, c=1), over, shift(over, c=1)), gains[0], space)
    away, up[2], down[2] = together(away, up[2], down[2])
    up.append(shift(up[2], z=1))
    down.append(shift(down[2], z=-1))
    came = shift(away, c=1)
    over = swap_chips((over + came[ROWS:]).astype(BF))
    over, up[3], down[3] = together(over, up[3], down[3])
    up.append(shift(up[3][:256], z=1))
    down.append(shift(down[3][256:], z=-1))
    first, normed = norm_call(base, came, over, gains[1])
    over = swap_chips(normed)
    mlp = (*down[:4], up[4], up[3], up[2], up[1], down[4])
    base, away, over = mlp_call(place, first, (normed, shift(normed, c=1), over, shift(over, c=1)), mlp)
    came = shift(away, c=1)
    over = swap_chips((over + came[ROWS:]).astype(BF))
    second = (base + came[:ROWS] + over.astype(F32)).astype(BF)

    groups = [[(2 * m + core) * 8 + k for m in range(16) for k in range(8)] for core in range(2)]
    series = lax.all_to_all(second, AXES, split_axis=0, concat_axis=0, tiled=True, axis_index_groups=groups)
    base, away = time_call(place, series, shift(series, c=1), gains[2], shared)
    done = leave_call(base, shift(away, c=1))
    return arrive_call(lax.all_to_all(done, "dp", split_axis=0, concat_axis=0, tiled=True))


def solution(mesh):
    return jax.shard_map(
        body,
        mesh=mesh,
        in_specs=(
            P(None, "dp", "fsdp", None),
            P(),
            P("fsdp", None),
            P("fsdp", None),
            P(),
            P("fsdp", None),
            P("fsdp", None),
            P(),
            P("fsdp", None),
            P("fsdp", None),
        ),
        out_specs=P(None, "dp", "fsdp", None),
        check_vma=False,
    )
```
